32 devices in a mesh: seq: 16 (over z, x, core), head: 2 (over y).
Axes of the slice: x: 2, y: 2, z: 4, core: 2. Of those that a mesh axis runs over, the one named last changes fastest.
Arguments:
- q_rot: bfloat16 [12288, 1024], P('seq', 'head'), may hold values from -6 to 6
- k_rot: bfloat16 [12288, 256], P('seq', 'head'), may hold values from -6 to 6
- values: bfloat16 [12288, 256], P('seq', 'head'), may hold values from -6 to 6
- attn_out: bfloat16 [12288, 1024], P('seq', 'head'), may hold values from -4 to 4
- out_grad: bfloat16 [12288, 1024], P('seq', 'head'), may hold values from -6 to 6
- log_norm: float32 [8, 12288], P('head', 'seq')
- stretch_ids: int32 [16, 2], replicated, may hold values from 0 to 31, as said below
- q_weight: bfloat16 [4096, 1024], P(None, 'head'), may hold values from -0.09375 to 0.09375
- k_weight: bfloat16 [4096, 256], P(None, 'head'), may hold values from -0.09375 to 0.09375
- v_weight: bfloat16 [4096, 256], P(None, 'head'), may hold values from -0.09375 to 0.09375
Outputs:
- d_input: bfloat16 [12288, 4096], P(('seq', 'head'))
- key_grad: bfloat16 [12288, 256], P('seq', 'head')
- value_grad: bfloat16 [12288, 256], P('seq', 'head')
The draws below stay inside these ranges and needn't reach their ends.
Inputs may be any that keep to these rules, and one draw needn't show every extreme that they name: `stretch_ids`: row j lists the two blocks of 384 consecutive positions whose tokens index j of seq holds, in its row order; every block appears once and the two entries of a row add up to 31.
All inputs are finite; a program needn't handle non-finite values.
Results may differ from the reference program's by a relative error of at most 0.0057.
Values may be sent and summed in bfloat16 or wider, within the bound.
A program may use at most 128 MiB of HBM per device.

```python
import math
import jax
import jax.numpy as jnp
from jax import lax

D = 4096
HD = 128
QH_DEV = 4
STOPS = 3
T_DEV = 768
BLOCK_LEN = 384
TOKENS = 12288
Q_HEADS = 8
KV_HEADS = 2
N_SEQ = 16


def block_pairs(key):
    block_count = TOKENS // T_DEV
    order_key, flip_key = jax.random.split(key)
    block_order = jax.random.permutation(order_key, block_count).astype(jnp.int32)
    flip_bits = jax.random.randint(flip_key, (block_count,), 0, 2, dtype=jnp.int32)
    late_ids = 2 * block_count - 1 - block_order
    first_ids = jnp.where(flip_bits == 1, late_ids, block_order)
    second_ids = jnp.where(flip_bits == 1, block_order, late_ids)
    return jnp.stack([first_ids, second_ids], axis=1)


def draw_stretch_ids(key, part):
    return block_pairs(key)


def draw_log_norm(key, part):
    stretch_pairs = block_pairs(key)
    key = jax.random.fold_in(key, 11)
    row_ids = jnp.arange(TOKENS, dtype=jnp.int32)
    slot_ids = stretch_pairs[row_ids // T_DEV, row_ids % T_DEV // BLOCK_LEN]
    positions = slot_ids * BLOCK_LEN + row_ids % BLOCK_LEN
    counted = jnp.minimum(positions.astype(jnp.float32) + 1.0, float(STOPS * T_DEV))
    spread = jax.random.uniform(key, (Q_HEADS, TOKENS), jnp.float32, -0.5, 0.5)
    return jnp.log(counted)[None, :] + 0.5 + spread


def block_scale(key, extent, pieces, smallest, high):
    def one(position, parts):
        heights = jax.random.uniform(jax.random.fold_in(jax.random.fold_in(key, 6), position), (parts,), jnp.float32, smallest / len(pieces), high / len(pieces))
        return jnp.repeat(jnp.exp(heights), extent[position] // parts).reshape((-1,) + (1,) * (len(extent) - position - 1))

    gain = one(*pieces[0])
    for cut in pieces[1:]:
        gain = gain * one(*cut)
    return gain


def noise(key, shape, scale, limit, cuts=(), held_as=jnp.bfloat16):
    entries = jax.random.normal(key, shape, jnp.float32) * scale
    if len(cuts) > 0:
        entries = block_scale(key, shape, cuts, -0.22, 0.18) * entries
    return jnp.clip(entries, min=-limit, max=limit).astype(held_as)


def setup_inputs(seed: int = 0) -> dict:
    seeds = jax.random.split(jax.random.key(seed), 11)
    return {
        "q_rot": noise(seeds[0], (TOKENS, Q_HEADS * HD), 1.0, 6.0, ((0, 16), (1, 2))),
        "k_rot": noise(seeds[1], (TOKENS, KV_HEADS * HD), 1.0, 6.0, ((0, 16), (1, 2))),
        "values": noise(seeds[2], (TOKENS, KV_HEADS * HD), 1.0, 6.0, ((0, 16), (1, 2))),
        "attn_out": noise(seeds[3], (TOKENS, Q_HEADS * HD), 0.3, 4.0, ((0, 16), (1, 2))),
        "out_grad": noise(seeds[4], (TOKENS, Q_HEADS * HD), 2.0, 6.0, ((0, 16), (1, 2))),
        "log_norm": draw_log_norm(jax.random.fold_in(seeds[10], 71), 0),
        "stretch_ids": draw_stretch_ids(jax.random.fold_in(seeds[10], 71), 0),
        "q_weight": noise(seeds[7], (D, Q_HEADS * HD), D ** -0.5, 0.09375, ((1, 2),)),
        "k_weight": noise(seeds[8], (D, KV_HEADS * HD), D ** -0.5, 0.09375, ((1, 2),)),
        "v_weight": noise(seeds[9], (D, KV_HEADS * HD), D ** -0.5, 0.09375, ((1, 2),)),
    }


def rotary_tables(positions, head_dim):
    half_dim = head_dim // 2
    inverse = jnp.exp(jnp.arange(half_dim, dtype=jnp.float32) * (-2.0 * math.log(500000.0) / head_dim))
    angles = positions.astype(jnp.float32)[:, None] * inverse[None, :]
    cosine_table = jnp.cos(angles)
    sine_table = jnp.sin(angles)
    return (jnp.concatenate([cosine_table, cosine_table], axis=1), jnp.concatenate([sine_table, sine_table], axis=1))

def unrotate(gradient, cosine_table, sine_table):
    half_dim = gradient.shape[-1] // 2
    rotated = gradient * sine_table
    return gradient * cosine_table + jnp.concatenate([rotated[..., half_dim:], -rotated[..., :half_dim]], axis=-1)

def reference(q_rot, k_rot, values, attn_out, out_grad, log_norm, stretch_ids, q_weight, k_weight, v_weight):
    row_ids = jnp.arange(TOKENS, dtype=jnp.int32)
    positions = (stretch_ids[row_ids // T_DEV, row_ids % T_DEV // BLOCK_LEN] * BLOCK_LEN + row_ids % BLOCK_LEN).astype(jnp.int32)
    score_scale = 1.0 / math.sqrt(HD)
    groups = KV_HEADS
    queries = q_rot.reshape(TOKENS, groups, QH_DEV, HD).transpose(1, 0, 2, 3)
    grads_out = out_grad.reshape(TOKENS, groups, QH_DEV, HD).transpose(1, 0, 2, 3)
    outputs = attn_out.reshape(TOKENS, groups, QH_DEV, HD).transpose(1, 0, 2, 3)
    key_rows = k_rot.reshape(TOKENS, groups, HD).transpose(1, 0, 2)
    value_rows = values.reshape(TOKENS, groups, HD).transpose(1, 0, 2)
    norm_table = log_norm.reshape(groups, QH_DEV, TOKENS)

    def per_group(operands):
        q_group, dout_group, out_group, k_group, v_group, norm_group = operands
        k_wide = k_group.astype(jnp.float32)
        v_wide = v_group.astype(jnp.float32)

        def per_block(loop_state, block_data):
            key_acc, value_acc = loop_state
            q_block, dout_block, out_block, norm_block, qpos_block, block_index = block_data
            q_wide = q_block.astype(jnp.float32)
            dout_wide = dout_block.astype(jnp.float32)
            delta_rows = lax.optimization_barrier(jnp.sum(dout_wide * out_block.astype(jnp.float32), axis=2)).T
            query_part = jnp.zeros((T_DEV, QH_DEV, HD), jnp.float32)
            for stop in range(STOPS):
                anchor = jnp.mod(block_index - stop, N_SEQ).astype(jnp.int32)
                start = (anchor * T_DEV).astype(jnp.int32)
                k_blk = lax.dynamic_slice_in_dim(k_wide, start, T_DEV, 0)
                v_blk = lax.dynamic_slice_in_dim(v_wide, start, T_DEV, 0)
                kpos = lax.dynamic_slice_in_dim(positions, start, T_DEV, 0)
                scores = jnp.einsum('thd,kd->htk', q_wide, k_blk) * score_scale
                visible = kpos[None, :] <= qpos_block[:, None]
                attn_probs = jnp.where(visible[None, :, :], jnp.exp(scores - norm_block[:, :, None]), 0.0)
                dprobs = jnp.einsum('thd,kd->htk', dout_wide, v_blk)
                dscores = lax.optimization_barrier((attn_probs * (dprobs - delta_rows[:, :, None])).astype(jnp.bfloat16)).astype(jnp.float32)
                probs_low = lax.optimization_barrier(attn_probs.astype(jnp.bfloat16)).astype(jnp.float32)
                value_term = jnp.einsum('htk,thd->kd', probs_low, dout_wide)
                key_term = jnp.einsum('htk,thd->kd', dscores, q_wide) * score_scale
                value_acc = lax.dynamic_update_slice_in_dim(value_acc, lax.dynamic_slice_in_dim(value_acc, start, T_DEV, 0) + value_term, start, 0)
                key_acc = lax.dynamic_update_slice_in_dim(key_acc, lax.dynamic_slice_in_dim(key_acc, start, T_DEV, 0) + key_term, start, 0)
                query_part = query_part + jnp.einsum('htk,kd->thd', dscores, k_blk) * score_scale
            return ((key_acc, value_acc), query_part)
        blocks = (q_group.reshape(N_SEQ, T_DEV, QH_DEV, HD), dout_group.reshape(N_SEQ, T_DEV, QH_DEV, HD), out_group.reshape(N_SEQ, T_DEV, QH_DEV, HD), norm_group.reshape(QH_DEV, N_SEQ, T_DEV).transpose(1, 0, 2), positions.reshape(N_SEQ, T_DEV), jnp.arange(N_SEQ, dtype=jnp.int32))
        start_state = (jnp.zeros((TOKENS, HD), jnp.float32), jnp.zeros((TOKENS, HD), jnp.float32))
        (key_raw, value_raw), query_blocks = lax.scan(per_block, start_state, blocks)
        return (query_blocks.reshape(TOKENS, QH_DEV, HD), key_raw, value_raw)
    query_raw, key_raw, value_raw = lax.map(per_group, (queries, grads_out, outputs, key_rows, value_rows, norm_table))
    cosine_table, sine_table = rotary_tables(positions, HD)
    query_grad = unrotate(query_raw.transpose(1, 0, 2, 3), cosine_table[:, None, None, :], sine_table[:, None, None, :])
    query_grad = query_grad.astype(jnp.bfloat16).reshape(TOKENS, Q_HEADS * HD)
    key_grad = unrotate(key_raw.transpose(1, 0, 2), cosine_table[:, None, :], sine_table[:, None, :])
    key_grad = key_grad.astype(jnp.bfloat16).reshape(TOKENS, KV_HEADS * HD)
    value_grad = value_raw.transpose(1, 0, 2).reshape(TOKENS, KV_HEADS * HD).astype(jnp.bfloat16)
    contract = (((1,), (1,)), ((), ()))
    d_input = lax.dot_general(query_grad, q_weight, contract, preferred_element_type=jnp.float32)
    d_input = d_input + lax.dot_general(key_grad, k_weight, contract, preferred_element_type=jnp.float32)
    d_input = d_input + lax.dot_general(value_grad, v_weight, contract, preferred_element_type=jnp.float32)
    return (d_input.astype(jnp.bfloat16), key_grad, value_grad)
```

```python
import functools
import math

import jax
import jax.numpy as jnp
from jax import lax
from jax.experimental import pallas as pl
from jax.experimental.pallas import tpu as pltpu
from jax.sharding import PartitionSpec as P

STOPS = 3
LOG2E = math.log2(math.e)
F32 = jnp.float32
BF16 = jnp.bfloat16
NT = (((1,), (1,)), ((), ()))
NN = (((1,), (0,)), ((), ()))
VMEM_LIMIT = 48 * 1024 * 1024


def dot(a, b, dims):
    return lax.dot_general(a, b, dims, preferred_element_type=F32)


def rotary_tables(positions, head_dim):
    half_dim = head_dim // 2
    inverse = jnp.exp(
        jnp.arange(half_dim, dtype=F32) * (-2.0 * math.log(500000.0) / head_dim)
    )
    angles = inverse[:, None] * positions.astype(F32)[None, :]
    return jnp.stack([jnp.cos(angles), jnp.sin(angles)])


def lo_half(ids_ref, row):
    first, second = ids_ref[row, 0], ids_ref[row, 1]
    swap = (second < first).astype(jnp.int32)
    return swap, jnp.minimum(first, second)


def attend(q_ref, do_ref, norm_ref, delta_ref, dq_ref, kv_block, k_acc, q_half, k_half, masked):
    half = norm_ref.shape[2]
    heads = norm_ref.shape[1]
    keys, vals = kv_block(k_half)
    hd = keys.shape[1]
    scale = LOG2E / math.sqrt(hd)
    keys_t = keys.T
    rows = pl.ds(pl.multiple_of(q_half * half, half), half)
    dk = jnp.zeros((half, hd), F32)
    dv = jnp.zeros((half, hd), F32)
    if masked:
        visible = lax.broadcasted_iota(jnp.int32, (half, half), 0) <= lax.broadcasted_iota(
            jnp.int32, (half, half), 1
        )
    for h in range(heads):
        cols = slice(h * hd, (h + 1) * hd)
        q = q_ref[rows, cols]
        do = do_ref[rows, cols]
        probs = jnp.exp2(dot(keys, q, NT) * scale - norm_ref[q_half, h : h + 1, :])
        if masked:
            probs = jnp.where(visible, probs, 0.0)
        ds = (probs * (dot(vals, do, NT) - delta_ref[q_half, h : h + 1, :])).astype(BF16)
        dv = dv + dot(probs.astype(BF16), do, NN)
        dk = dk + dot(ds, q, NN)
        dq_ref[q_half, cols, :] += dot(keys_t, ds, NN)
    k_acc[k_half, :, :hd] += dk
    k_acc[k_half, :, hd:] += dv


def own_kernel(seq_count, ids_ref, q_ref, k_ref, v_ref, o_ref, do_ref, ln_ref, dq_ref, kv_ref, norm_ref, delta_ref):
    me = lax.axis_index("seq")
    heads, half = norm_ref.shape[1:]
    hd = k_ref.shape[1]
    for h in range(heads):
        cols = slice(h * hd, (h + 1) * hd)
        prod = do_ref[:, cols].astype(F32) * o_ref[:, cols].astype(F32)
        delta = jnp.sum(prod.T, axis=0, keepdims=True)
        for a in range(2):
            delta_ref[a, h : h + 1, :] = delta[:, a * half : (a + 1) * half]
    for a in range(2):
        norm_ref[a] = ln_ref[:, a * half : (a + 1) * half] * LOG2E
    dq_ref[...] = jnp.zeros_like(dq_ref)
    kv_ref[...] = jnp.zeros_like(kv_ref)

    def kv_block(b):
        rows = pl.ds(pl.multiple_of(b * half, half), half)
        return k_ref[rows, :], v_ref[rows, :]

    run = functools.partial(attend, q_ref, do_ref, norm_ref, delta_ref, dq_ref, kv_block, kv_ref)
    run(0, 0, True)
    run(1, 1, True)
    lo, _ = lo_half(ids_ref, me)
    run(1 - lo, lo, False)


def far_kernel(seq_count, ids_ref, q_ref, do_ref, norm_ref, delta_ref, dq0_ref, tab_ref, *rest):
    stops = STOPS - 1
    kv_refs, qg_ref, home_refs = rest[:stops], rest[stops], rest[stops + 1 : 2 * stops + 1]
    dq_ref, acc_ref = rest[2 * stops + 1 :]
    me = lax.axis_index("seq")
    heads, half = norm_ref.shape[1:]
    hd = kv_refs[0].shape[1] // 2
    dq_ref[...] = dq0_ref[...]
    lo, low_id = lo_half(ids_ref, me)
    for i in range(stops):
        kv_ref, acc = kv_refs[i], acc_ref.at[i]
        acc[...] = jnp.zeros_like(acc)
        row = lax.rem(me - (i + 1) + seq_count, seq_count)
        k_lo, k_low_id = lo_half(ids_ref, row)

        def kv_block(b, kv_ref=kv_ref):
            rows = pl.ds(pl.multiple_of(b * half, half), half)
            return kv_ref[rows, :hd], kv_ref[rows, hd:]

        run = functools.partial(attend, q_ref, do_ref, norm_ref, delta_ref, dq_ref, kv_block, acc)
        run(1 - lo, k_lo, False)
        lows = k_low_id < low_id
        run(jnp.where(lows, lo, 1 - lo), jnp.where(lows, k_lo, 1 - k_lo), False)
        for b in range(2):
            home_refs[i][b * half : (b + 1) * half, :] = acc[b].astype(BF16)
    scale = 1.0 / math.sqrt(hd)
    hh = hd // 2
    for a in range(2):
        cos = tab_ref[0, :, a * half : (a + 1) * half] * scale
        sin = tab_ref[1, :, a * half : (a + 1) * half] * scale
        for h in range(heads):
            first = dq_ref[a, h * hd : h * hd + hh, :]
            second = dq_ref[a, h * hd + hh : (h + 1) * hd, :]
            turned = jnp.concatenate(
                [first * cos + second * sin, second * cos - first * sin], axis=0
            )
            qg_ref[a * half : (a + 1) * half, h * hd : (h + 1) * hd] = turned.T.astype(BF16)


def finish_kernel(tab_ref, kv0_ref, *rest):
    home_refs, (kg_ref, vg_ref) = rest[:-2], rest[-2:]
    half = kv0_ref.shape[1]
    hd = kg_ref.shape[1]
    hh = hd // 2
    scale = 1.0 / math.sqrt(hd)
    for a in range(2):
        rows = slice(a * half, (a + 1) * half)
        total = kv0_ref[a]
        for ref in home_refs:
            total = total + ref[rows, :].astype(F32)
        cos = tab_ref[0, :, rows]
        sin = tab_ref[1, :, rows]
        cos = jnp.concatenate([cos, cos], axis=0).T * scale
        sin = jnp.concatenate([sin, -sin], axis=0).T * scale
        dk = total[:, :hd]
        swapped = jnp.concatenate([dk[:, hh:], dk[:, :hh]], axis=1)
        kg_ref[rows, :] = (dk * cos + swapped * sin).astype(BF16)
        vg_ref[rows, :] = total[:, hd:].astype(BF16)


def project_kernel(others, slots, r_ref, qg, kg, vg, qo, kvo, wq, wk, wv, p0, p1, p2, p3, out_ref, buf, sem):
    j = pl.program_id(0)
    pieces = (p0, p1, p2, p3)
    qw, kw = qg.shape[1], kg.shape[1]

    def copy(i):
        return pltpu.make_async_copy(pieces[i], buf.at[i % slots], sem.at[i])

    for i in range(4):
        @pl.when(j == max(0, i - slots + 1))
        def _(i=i):
            copy(i).start()

    total = dot(qg[...], wq[...], NT) + dot(kg[...], wk[...], NT) + dot(vg[...], wv[...], NT)
    for i in range(4):
        @pl.when(j == i)
        def _(i=i):
            copy(i).wait()

    slot = lax.rem(j, slots)
    width = qw + 2 * kw
    for s in range(others):
        total = total + dot(
            qo[:, s * qw : (s + 1) * qw], buf[slot, :, s * width : s * width + qw], NT
        )
        total = total + dot(
            kvo[:, s * 2 * kw : (s + 1) * 2 * kw],
            buf[slot, :, s * width + qw : (s + 1) * width],
            NT,
        )
    out_ref[...] = total.astype(BF16)


def params(**kw):
    return pltpu.CompilerParams(vmem_limit_bytes=VMEM_LIMIT, **kw)


def local(
    q_rot, k_rot, values, attn_out, out_grad, log_norm, stretch_ids, q_weight, k_weight, v_weight
):
    seq_count = lax.axis_size("seq")
    head_axis = lax.axis_size("head")
    tok, col_width = q_rot.shape
    hd = k_rot.shape[1]
    heads = col_width // hd
    half = tok // 2
    d_model = q_weight.shape[0]
    me = lax.axis_index("seq")
    my_head = lax.axis_index("head")
    quarter = d_model // 4
    part = lax.rem(me, 4)

    def shift_seq(x, by):
        return lax.ppermute(x, "seq", [(i, (i + by) % seq_count) for i in range(seq_count)])

    def swap_seq(x, bit):
        return lax.ppermute(x, "seq", [(i, i ^ bit) for i in range(seq_count)])

    def from_head(x, by):
        return lax.ppermute(x, "head", [(i, (i - by) % head_axis) for i in range(head_axis)])

    kv = jnp.concatenate([k_rot, values], axis=1)
    kvs = [shift_seq(kv, stop) for stop in range(1, STOPS)]

    def rows_of(w):
        return lax.dynamic_slice_in_dim(w, part * quarter, quarter, 0)

    mine = jnp.concatenate([rows_of(q_weight), rows_of(k_weight), rows_of(v_weight)], axis=1)
    got = [from_head(mine, s) for s in range(1, head_axis)]
    piece0 = got[0] if len(got) == 1 else jnp.concatenate(got, axis=1)
    piece2 = swap_seq(piece0, 2)
    piece1 = swap_seq(piece0, 1)
    piece3 = swap_seq(piece2, 1)

    own_ids = lax.dynamic_index_in_dim(stretch_ids, me, 0, keepdims=False)
    offsets = jnp.arange(half, dtype=jnp.int32)
    positions = (own_ids[:, None] * half + offsets[None, :]).reshape(tok)
    tables = rotary_tables(positions, hd)

    smem = pl.BlockSpec(memory_space=pltpu.SMEM)
    vmem = pl.BlockSpec(memory_space=pltpu.VMEM)
    unit = 10 * heads * half * half * hd
    dq0, kv0, norm, delta = pl.pallas_call(
        functools.partial(own_kernel, seq_count),
        out_shape=(
            jax.ShapeDtypeStruct((2, col_width, half), F32),
            jax.ShapeDtypeStruct((2, half, 2 * hd), F32),
            jax.ShapeDtypeStruct((2, heads, half), F32),
            jax.ShapeDtypeStruct((2, heads, half), F32),
        ),
        in_specs=[smem] + [vmem] * 6,
        out_specs=(vmem,) * 4,
        compiler_params=params(),
        cost_estimate=pl.CostEstimate(
            flops=3 * unit, bytes_accessed=5 * 2**20, transcendentals=3 * heads * half * half
        ),
        name="own_stop",
    )(stretch_ids, q_rot, k_rot, values, attn_out, out_grad, log_norm)

    query_grad, *homes = pl.pallas_call(
        functools.partial(far_kernel, seq_count),
        out_shape=(jax.ShapeDtypeStruct((tok, col_width), BF16),)
        + (jax.ShapeDtypeStruct((tok, 2 * hd), BF16),) * (STOPS - 1),
        in_specs=[smem] + [vmem] * (6 + STOPS - 1),
        out_specs=(vmem,) * STOPS,
        scratch_shapes=[
            pltpu.VMEM((2, col_width, half), F32),
            pltpu.VMEM((STOPS - 1, 2, half, 2 * hd), F32),
        ],
        compiler_params=params(),
        cost_estimate=pl.CostEstimate(
            flops=4 * unit, bytes_accessed=6 * 2**20, transcendentals=4 * heads * half * half
        ),
        name="far_stops",
    )(stretch_ids, q_rot, out_grad, norm, delta, dq0, tables, *kvs)

    homes = [shift_seq(x, -(i + 1)) for i, x in enumerate(homes)]
    out_rows = tok // head_axis

    def rows_for(x, h):
        return lax.dynamic_slice_in_dim(x, lax.rem(h, head_axis) * out_rows, out_rows, 0)

    def exchange(x):
        got = [
            from_head(rows_for(x, my_head + head_axis - s), s) for s in range(1, head_axis)
        ]
        return got[0] if len(got) == 1 else jnp.concatenate(got, axis=1)

    q_other = exchange(query_grad)
    key_grad, value_grad = pl.pallas_call(
        finish_kernel,
        out_shape=(jax.ShapeDtypeStruct((tok, hd), BF16),) * 2,
        in_specs=[vmem] * (1 + STOPS),
        out_specs=(vmem,) * 2,
        compiler_params=params(),
        name="finish_keys",
    )(tables, kv0, *homes)
    kv_other = exchange(jnp.concatenate([key_grad, value_grad], axis=1))

    others = head_axis - 1
    slots = 4 if others == 1 else 2
    full = lambda shape: pl.BlockSpec(shape, lambda j, r: (0, 0))
    wspec = lambda cols: pl.BlockSpec((quarter, cols), lambda j, r: (r[0] ^ j, 0))
    hbm = pl.BlockSpec(memory_space=pl.ANY)
    d_input = pl.pallas_call(
        functools.partial(project_kernel, others, slots),
        out_shape=jax.ShapeDtypeStruct((out_rows, d_model), BF16),
        grid_spec=pltpu.PrefetchScalarGridSpec(
            num_scalar_prefetch=1,
            grid=(4,),
            in_specs=[
                full((out_rows, col_width)),
                full((out_rows, hd)),
                full((out_rows, hd)),
                full((out_rows, col_width * others)),
                full((out_rows, 2 * hd * others)),
                wspec(col_width),
                wspec(hd),
                wspec(hd),
                hbm,
                hbm,
                hbm,
                hbm,
            ],
            out_specs=pl.BlockSpec((out_rows, quarter), lambda j, r: (0, r[0] ^ j)),
            scratch_shapes=[
                pltpu.VMEM((slots, quarter, (col_width + 2 * hd) * others), BF16),
                pltpu.SemaphoreType.DMA((4,)),
            ],
        ),
        compiler_params=params(),
        name="project",
    )(
        part.reshape(1),
        rows_for(query_grad, my_head),
        rows_for(key_grad, my_head),
        rows_for(value_grad, my_head),
        q_other,
        kv_other,
        q_weight,
        k_weight,
        v_weight,
        piece0,
        piece1,
        piece2,
        piece3,
    )
    return (d_input, key_grad, value_grad)


def solution(mesh):
    in_specs = (
        P("seq", "head"),
        P("seq", "head"),
        P("seq", "head"),
        P("seq", "head"),
        P("seq", "head"),
        P("head", "seq"),
        P(),
        P(None, "head"),
        P(None, "head"),
        P(None, "head"),
    )
    out_specs = (P(("seq", "head"), None), P("seq", "head"), P("seq", "head"))
    return jax.shard_map(local, mesh=mesh, in_specs=in_specs, out_specs=out_specs, check_vma=False)
```

```python
import functools
import math

import jax
import jax.numpy as jnp
from jax import lax
from jax.experimental import pallas as pl
from jax.experimental.pallas import tpu as pltpu
from jax.sharding import PartitionSpec as P

STOPS = 3
LOG2E = math.log2(math.e)
F32 = jnp.float32
BF16 = jnp.bfloat16
NT = (((1,), (1,)), ((), ()))
NN = (((1,), (0,)), ((), ()))
VMEM_LIMIT = 48 * 1024 * 1024


def dot(a, b, dims):
    return lax.dot_general(a, b, dims, preferred_element_type=F32)


def rotary_tables(positions, head_dim):
    half_dim = head_dim // 2
    inverse = jnp.exp(
        jnp.arange(half_dim, dtype=F32) * (-2.0 * math.log(500000.0) / head_dim)
    )
    angles = inverse[:, None] * positions.astype(F32)[None, :]
    return jnp.stack([jnp.cos(angles), jnp.sin(angles)])


def lo_half(ids_ref, row):
    first, second = ids_ref[row, 0], ids_ref[row, 1]
    swap = (second < first).astype(jnp.int32)
    return swap, jnp.minimum(first, second)


def attend(q_ref, do_ref, norm_ref, delta_ref, dq_ref, kv_block, k_acc, q_half, k_half, masked):
    half = norm_ref.shape[2]
    heads = norm_ref.shape[1]
    keys, vals = kv_block(k_half)
    hd = keys.shape[1]
    scale = LOG2E / math.sqrt(hd)
    keys_t = keys.T
    rows = pl.ds(pl.multiple_of(q_half * half, half), half)
    dk = jnp.zeros((half, hd), F32)
    dv = jnp.zeros((half, hd), F32)
    if masked:
        visible = lax.broadcasted_iota(jnp.int32, (half, half), 0) <= lax.broadcasted_iota(
            jnp.int32, (half, half), 1
        )
    for h in range(heads):
        cols = slice(h * hd, (h + 1) * hd)
        q = q_ref[rows, cols]
        do = do_ref[rows, cols]
        probs = jnp.exp2(dot(keys, q, NT) * scale - norm_ref[q_half, h : h + 1, :])
        if masked:
            probs = jnp.where(visible, probs, 0.0)
        ds = (probs * (dot(vals, do, NT) - delta_ref[q_half, h : h + 1, :])).astype(BF16)
        dv = dv + dot(probs.astype(BF16), do, NN)
        dk = dk + dot(ds, q, NN)
        dq_ref[q_half, cols, :] += dot(keys_t, ds, NN)
    k_acc[k_half, :, :hd] += dk
    k_acc[k_half, :, hd:] += dv


def own_kernel(seq_count, ids_ref, q_ref, k_ref, v_ref, o_ref, do_ref, ln_ref, dq_ref, kv_ref, norm_ref, delta_ref):
    me = lax.axis_index("seq")
    heads, half = norm_ref.shape[1:]
    hd = k_ref.shape[1]
    for h in range(heads):
        cols = slice(h * hd, (h + 1) * hd)
        prod = do_ref[:, cols].astype(F32) * o_ref[:, cols].astype(F32)
        delta = jnp.sum(prod.T, axis=0, keepdims=True)
        for a in range(2):
            delta_ref[a, h : h + 1, :] = delta[:, a * half : (a + 1) * half]
    for a in range(2):
        norm_ref[a] = ln_ref[:, a * half : (a + 1) * half] * LOG2E
    dq_ref[...] = jnp.zeros_like(dq_ref)
    kv_ref[...] = jnp.zeros_like(kv_ref)

    def kv_block(b):
        rows = pl.ds(pl.multiple_of(b * half, half), half)
        return k_ref[rows, :], v_ref[rows, :]

    run = functools.partial(attend, q_ref, do_ref, norm_ref, delta_ref, dq_ref, kv_block, kv_ref)
    run(0, 0, True)
    run(1, 1, True)
    lo, _ = lo_half(ids_ref, me)
    run(1 - lo, lo, False)


def far_kernel(seq_count, ids_ref, q_ref, do_ref, norm_ref, delta_ref, dq0_ref, tab_ref, *rest):
    stops = STOPS - 1
    kv_refs, qg_ref, home_refs = rest[:stops], rest[stops], rest[stops + 1 : 2 * stops + 1]
    dq_ref, acc_ref = rest[2 * stops + 1 :]
    me = lax.axis_index("seq")
    heads, half = norm_ref.shape[1:]
    hd = kv_refs[0].shape[1] // 2
    dq_ref[...] = dq0_ref[...]
    lo, low_id = lo_half(ids_ref, me)
    for i in range(stops):
        kv_ref, acc = kv_refs[i], acc_ref.at[i]
        acc[...] = jnp.zeros_like(acc)
        row = lax.rem(me - (i + 1) + seq_count, seq_count)
        k_lo, k_low_id = lo_half(ids_ref, row)

        def kv_block(b, kv_ref=kv_ref):
            rows = pl.ds(pl.multiple_of(b * half, half), half)
            return kv_ref[rows, :hd], kv_ref[rows, hd:]

        run = functools.partial(attend, q_ref, do_ref, norm_ref, delta_ref, dq_ref, kv_block, acc)
        run(1 - lo, k_lo, False)
        lows = k_low_id < low_id
        run(jnp.where(lows, lo, 1 - lo), jnp.where(lows, k_lo, 1 - k_lo), False)
        for b in range(2):
            home_refs[i][b * half : (b + 1) * half, :] = acc[b].astype(BF16)
    scale = 1.0 / math.sqrt(hd)
    hh = hd // 2
    for a in range(2):
        cos = tab_ref[0, :, a * half : (a + 1) * half] * scale
        sin = tab_ref[1, :, a * half : (a + 1) * half] * scale
        for h in range(heads):
            first = dq_ref[a, h * hd : h * hd + hh, :]
            second = dq_ref[a, h * hd + hh : (h + 1) * hd, :]
            turned = jnp.concatenate(
                [first * cos + second * sin, second * cos - first * sin], axis=0
            )
            qg_ref[a * half : (a + 1) * half, h * hd : (h + 1) * hd] = turned.T.astype(BF16)


def finish_kernel(tab_ref, kv0_ref, *rest):
    home_refs, (kg_ref, vg_ref) = rest[:-2], rest[-2:]
    half = kv0_ref.shape[1]
    hd = kg_ref.shape[1]
    hh = hd // 2
    scale = 1.0 / math.sqrt(hd)
    for a in range(2):
        rows = slice(a * half, (a + 1) * half)
        total = kv0_ref[a]
        for ref in home_refs:
            total = total + ref[rows, :].astype(F32)
        cos = tab_ref[0, :, rows]
        sin = tab_ref[1, :, rows]
        cos = jnp.concatenate([cos, cos], axis=0).T * scale
        sin = jnp.concatenate([sin, -sin], axis=0).T * scale
        dk = total[:, :hd]
        swapped = jnp.concatenate([dk[:, hh:], dk[:, :hh]], axis=1)
        kg_ref[rows, :] = (dk * cos + swapped * sin).astype(BF16)
        vg_ref[rows, :] = total[:, hd:].astype(BF16)


def project_kernel(others, slots, r_ref, qg, kg, vg, qo, kvo, wq, wk, wv, *rest):
    j = pl.program_id(0)
    pieces, (out_ref, buf, sem) = rest[:8], rest[8:]
    qw, kw = qg.shape[1], kg.shape[1]

    def copy(i):
        return pltpu.make_async_copy(pieces[i], buf.at[i % slots], sem.at[i])

    for i in range(8):
        @pl.when(j == max(0, i - slots + 1))
        def _(i=i):
            copy(i).start()

    total = dot(qg[...], wq[...], NT) + dot(kg[...], wk[...], NT) + dot(vg[...], wv[...], NT)
    for i in range(8):
        @pl.when(j == i)
        def _(i=i):
            copy(i).wait()

    slot = lax.rem(j, slots)
    width = qw + 2 * kw
    for s in range(others):
        total = total + dot(
            qo[:, s * qw : (s + 1) * qw], buf[slot, :, s * width : s * width + qw], NT
        )
        total = total + dot(
            kvo[:, s * 2 * kw : (s + 1) * 2 * kw],
            buf[slot, :, s * width + qw : (s + 1) * width],
            NT,
        )
    out_ref[...] = total.astype(BF16)


def tie_kernel(*refs):
    pass


def tie(arrays, after):
    hbm = pl.BlockSpec(memory_space=pl.ANY)
    return pl.pallas_call(
        tie_kernel,
        out_shape=tuple(jax.ShapeDtypeStruct(x.shape, x.dtype) for x in arrays),
        in_specs=[hbm] * (len(arrays) + 1),
        out_specs=(hbm,) * len(arrays),
        input_output_aliases={i: i for i in range(len(arrays))},
        name="tie",
    )(*arrays, after)


def params(**kw):
    return pltpu.CompilerParams(vmem_limit_bytes=VMEM_LIMIT, **kw)


def local(
    q_rot, k_rot, values, attn_out, out_grad, log_norm, stretch_ids, q_weight, k_weight, v_weight
):
    seq_count = lax.axis_size("seq")
    head_axis = lax.axis_size("head")
    tok, col_width = q_rot.shape
    hd = k_rot.shape[1]
    heads = col_width // hd
    half = tok // 2
    d_model = q_weight.shape[0]
    me = lax.axis_index("seq")
    my_head = lax.axis_index("head")
    eighth = d_model // 8
    part = lax.rem(me, 8)

    def shift_seq(x, by):
        return lax.ppermute(x, "seq", [(i, (i + by) % seq_count) for i in range(seq_count)])

    def swap_seq(x, bit):
        return lax.ppermute(x, "seq", [(i, i ^ bit) for i in range(seq_count)])

    def from_head(x, by):
        return lax.ppermute(x, "head", [(i, (i - by) % head_axis) for i in range(head_axis)])

    kv = jnp.concatenate([k_rot, values], axis=1)
    kvs = [shift_seq(kv, stop) for stop in range(1, STOPS)]

    def piece_of(which):
        def rows_of(w):
            return lax.dynamic_slice_in_dim(w, which * eighth, eighth, 0)

        return jnp.concatenate([rows_of(q_weight), rows_of(k_weight), rows_of(v_weight)], axis=1)

    def fetch(x):
        got = [from_head(x, s) for s in range(1, head_axis)]
        return got[0] if len(got) == 1 else jnp.concatenate(got, axis=1)

    near = fetch(piece_of(part))
    later = piece_of(part ^ 6)

    own_ids = lax.dynamic_index_in_dim(stretch_ids, me, 0, keepdims=False)
    offsets = jnp.arange(half, dtype=jnp.int32)
    positions = (own_ids[:, None] * half + offsets[None, :]).reshape(tok)
    tables = rotary_tables(positions, hd)

    smem = pl.BlockSpec(memory_space=pltpu.SMEM)
    vmem = pl.BlockSpec(memory_space=pltpu.VMEM)
    unit = 10 * heads * half * half * hd
    dq0, kv0, norm, delta = pl.pallas_call(
        functools.partial(own_kernel, seq_count),
        out_shape=(
            jax.ShapeDtypeStruct((2, col_width, half), F32),
            jax.ShapeDtypeStruct((2, half, 2 * hd), F32),
            jax.ShapeDtypeStruct((2, heads, half), F32),
            jax.ShapeDtypeStruct((2, heads, half), F32),
        ),
        in_specs=[smem] + [vmem] * 6,
        out_specs=(vmem,) * 4,
        compiler_params=params(),
        cost_estimate=pl.CostEstimate(
            flops=3 * unit, bytes_accessed=5 * 2**20, transcendentals=3 * heads * half * half
        ),
        name="own_stop",
    )(stretch_ids, q_rot, k_rot, values, attn_out, out_grad, log_norm)

    near, later = tie((near, later), norm)
    over_x = swap_seq(near, 2)
    over_z = swap_seq(near, 4)
    over_y = fetch(later)
    near_twin = swap_seq(near, 1)

    query_grad, *homes = pl.pallas_call(
        functools.partial(far_kernel, seq_count),
        out_shape=(jax.ShapeDtypeStruct((tok, col_width), BF16),)
        + (jax.ShapeDtypeStruct((tok, 2 * hd), BF16),) * (STOPS - 1),
        in_specs=[smem] + [vmem] * (6 + STOPS - 1),
        out_specs=(vmem,) * STOPS,
        scratch_shapes=[
            pltpu.VMEM((2, col_width, half), F32),
            pltpu.VMEM((STOPS - 1, 2, half, 2 * hd), F32),
        ],
        compiler_params=params(),
        cost_estimate=pl.CostEstimate(
            flops=4 * unit, bytes_accessed=6 * 2**20, transcendentals=4 * heads * half * half
        ),
        name="far_stops",
    )(stretch_ids, q_rot, out_grad, norm, delta, dq0, tables, *kvs)

    over_x, over_z, over_y = tie((over_x, over_z, over_y), homes[0])
    pieces = [near, over_x, over_z, over_y, near_twin]
    pieces += [swap_seq(x, 1) for x in (over_x, over_z, over_y)]
    homes = [shift_seq(x, -(i + 1)) for i, x in enumerate(homes)]
    out_rows = tok // head_axis

    def rows_for(x, h):
        return lax.dynamic_slice_in_dim(x, lax.rem(h, head_axis) * out_rows, out_rows, 0)

    def exchange(x):
        got = [
            from_head(rows_for(x, my_head + head_axis - s), s) for s in range(1, head_axis)
        ]
        return got[0] if len(got) == 1 else jnp.concatenate(got, axis=1)

    q_other = exchange(query_grad)
    key_grad, value_grad = pl.pallas_call(
        finish_kernel,
        out_shape=(jax.ShapeDtypeStruct((tok, hd), BF16),) * 2,
        in_specs=[vmem] * (1 + STOPS),
        out_specs=(vmem,) * 2,
        compiler_params=params(),
        name="finish_keys",
    )(tables, kv0, *homes)
    kv_other = exchange(jnp.concatenate([key_grad, value_grad], axis=1))

    others = head_axis - 1
    slots = 8 if others == 1 else 2
    full = lambda shape: pl.BlockSpec(shape, lambda j, r: (0, 0))
    which = lambda j, r: r[0] ^ (2 * (j % 4) + j // 4)
    wspec = lambda cols: pl.BlockSpec((eighth, cols), lambda j, r: (which(j, r), 0))
    hbm = pl.BlockSpec(memory_space=pl.ANY)
    d_input = pl.pallas_call(
        functools.partial(project_kernel, others, slots),
        out_shape=jax.ShapeDtypeStruct((out_rows, d_model), BF16),
        grid_spec=pltpu.PrefetchScalarGridSpec(
            num_scalar_prefetch=1,
            grid=(8,),
            in_specs=[
                full((out_rows, col_width)),
                full((out_rows, hd)),
                full((out_rows, hd)),
                full((out_rows, col_width * others)),
                full((out_rows, 2 * hd * others)),
                wspec(col_width),
                wspec(hd),
                wspec(hd),
            ]
            + [hbm] * 8,
            out_specs=pl.BlockSpec((out_rows, eighth), lambda j, r: (0, which(j, r))),
            scratch_shapes=[
                pltpu.VMEM((slots, eighth, (col_width + 2 * hd) * others), BF16),
                pltpu.SemaphoreType.DMA((8,)),
            ],
        ),
        compiler_params=params(),
        name="project",
    )(
        part.reshape(1),
        rows_for(query_grad, my_head),
        rows_for(key_grad, my_head),
        rows_for(value_grad, my_head),
        q_other,
        kv_other,
        q_weight,
        k_weight,
        v_weight,
        *pieces,
    )
    return (d_input, key_grad, value_grad)


def solution(mesh):
    in_specs = (
        P("seq", "head"),
        P("seq", "head"),
        P("seq", "head"),
        P("seq", "head"),
        P("seq", "head"),
        P("head", "seq"),
        P(),
        P(None, "head"),
        P(None, "head"),
        P(None, "head"),
    )
    out_specs = (P(("seq", "head"), None), P("seq", "head"), P("seq", "head"))
    return jax.shard_map(local, mesh=mesh, in_specs=in_specs, out_specs=out_specs, check_vma=False)
```

```python
import functools
import math

import jax
import jax.numpy as jnp
from jax import lax
from jax.experimental import pallas as pl
from jax.experimental.pallas import tpu as pltpu
from jax.sharding import PartitionSpec as P

STOPS = 3
LOG2E = math.log2(math.e)
F32 = jnp.float32
BF16 = jnp.bfloat16
NT = (((1,), (1,)), ((), ()))
NN = (((1,), (0,)), ((), ()))
VMEM_LIMIT = 127 * 512 * 1024


def dot(a, b, dims):
    return lax.dot_general(a, b, dims, preferred_element_type=F32)


def rotary_tables(positions, head_dim):
    half_dim = head_dim // 2
    inverse = jnp.exp(
        jnp.arange(half_dim, dtype=F32) * (-2.0 * math.log(500000.0) / head_dim)
    )
    angles = inverse[:, None] * positions.astype(F32)[None, :]
    return jnp.stack([jnp.cos(angles), jnp.sin(angles)])


def lo_half(ids_ref, row):
    first, second = ids_ref[row, 0], ids_ref[row, 1]
    swap = (second < first).astype(jnp.int32)
    return swap, jnp.minimum(first, second)


def attend(q_ref, do_ref, norm_ref, delta_ref, dq_ref, kv_block, k_acc, q_half, k_half, masked):
    half = norm_ref.shape[2]
    heads = norm_ref.shape[1]
    keys, vals = kv_block(k_half)
    hd = keys.shape[1]
    scale = LOG2E / math.sqrt(hd)
    keys_t = keys.T
    rows = pl.ds(pl.multiple_of(q_half * half, half), half)
    dk = jnp.zeros((half, hd), F32)
    dv = jnp.zeros((half, hd), F32)
    if masked:
        visible = lax.broadcasted_iota(jnp.int32, (half, half), 0) <= lax.broadcasted_iota(
            jnp.int32, (half, half), 1
        )
    for h in range(heads):
        cols = slice(h * hd, (h + 1) * hd)
        q = q_ref[rows, cols]
        do = do_ref[rows, cols]
        probs = jnp.exp2(dot(keys, q, NT) * scale - norm_ref[q_half, h : h + 1, :])
        if masked:
            probs = jnp.where(visible, probs, 0.0)
        ds = (probs * (dot(vals, do, NT) - delta_ref[q_half, h : h + 1, :])).astype(BF16)
        dv = dv + dot(probs.astype(BF16), do, NN)
        dk = dk + dot(ds, q, NN)
        dq_ref[q_half, cols, :] += dot(keys_t, ds, NN)
    k_acc[k_half, :, :hd] += dk
    k_acc[k_half, :, hd:] += dv


def own_kernel(seq_count, ids_ref, q_ref, k_ref, v_ref, o_ref, do_ref, ln_ref, dq_ref, kv_ref, norm_ref, delta_ref):
    me = lax.axis_index("seq")
    heads, half = norm_ref.shape[1:]
    hd = k_ref.shape[1]
    for h in range(heads):
        cols = slice(h * hd, (h + 1) * hd)
        prod = do_ref[:, cols].astype(F32) * o_ref[:, cols].astype(F32)
        delta = jnp.sum(prod.T, axis=0, keepdims=True)
        for a in range(2):
            delta_ref[a, h : h + 1, :] = delta[:, a * half : (a + 1) * half]
    for a in range(2):
        norm_ref[a] = ln_ref[:, a * half : (a + 1) * half] * LOG2E
    dq_ref[...] = jnp.zeros_like(dq_ref)
    kv_ref[...] = jnp.zeros_like(kv_ref)

    def kv_block(b):
        rows = pl.ds(pl.multiple_of(b * half, half), half)
        return k_ref[rows, :], v_ref[rows, :]

    run = functools.partial(attend, q_ref, do_ref, norm_ref, delta_ref, dq_ref, kv_block, kv_ref)
    run(0, 0, True)
    run(1, 1, True)
    lo, _ = lo_half(ids_ref, me)
    run(1 - lo, lo, False)


def far_kernel(seq_count, ids_ref, q_ref, do_ref, norm_ref, delta_ref, dq0_ref, tab_ref, *rest):
    stops = STOPS - 1
    kv_refs, qg_ref, home_refs = rest[:stops], rest[stops], rest[stops + 1 : 2 * stops + 1]
    dq_ref, acc_ref = rest[2 * stops + 1 :]
    me = lax.axis_index("seq")
    heads, half = norm_ref.shape[1:]
    hd = kv_refs[0].shape[1] // 2
    dq_ref[...] = dq0_ref[...]
    lo, low_id = lo_half(ids_ref, me)
    for i in range(stops):
        kv_ref, acc = kv_refs[i], acc_ref.at[i]
        acc[...] = jnp.zeros_like(acc)
        row = lax.rem(me - (i + 1) + seq_count, seq_count)
        k_lo, k_low_id = lo_half(ids_ref, row)

        def kv_block(b, kv_ref=kv_ref):
            rows = pl.ds(pl.multiple_of(b * half, half), half)
            return kv_ref[rows, :hd], kv_ref[rows, hd:]

        run = functools.partial(attend, q_ref, do_ref, norm_ref, delta_ref, dq_ref, kv_block, acc)
        run(1 - lo, k_lo, False)
        lows = k_low_id < low_id
        run(jnp.where(lows, lo, 1 - lo), jnp.where(lows, k_lo, 1 - k_lo), False)
        for b in range(2):
            home_refs[i][b * half : (b + 1) * half, :] = acc[b].astype(BF16)
    scale = 1.0 / math.sqrt(hd)
    hh = hd // 2
    for a in range(2):
        cos = tab_ref[0, :, a * half : (a + 1) * half] * scale
        sin = tab_ref[1, :, a * half : (a + 1) * half] * scale
        for h in range(heads):
            first = dq_ref[a, h * hd : h * hd + hh, :]
            second = dq_ref[a, h * hd + hh : (h + 1) * hd, :]
            turned = jnp.concatenate(
                [first * cos + second * sin, second * cos - first * sin], axis=0
            )
            qg_ref[a * half : (a + 1) * half, h * hd : (h + 1) * hd] = turned.T.astype(BF16)


def finish_kernel(tab_ref, kv0_ref, after_ref, *rest):
    home_refs, (kg_ref, vg_ref, both_ref) = rest[:-3], rest[-3:]
    half = kv0_ref.shape[1]
    hd = kg_ref.shape[1]
    hh = hd // 2
    scale = 1.0 / math.sqrt(hd)
    for a in range(2):
        rows = slice(a * half, (a + 1) * half)
        total = kv0_ref[a]
        for ref in home_refs:
            total = total + ref[rows, :].astype(F32)
        cos = tab_ref[0, :, rows]
        sin = tab_ref[1, :, rows]
        cos = jnp.concatenate([cos, cos], axis=0).T * scale
        sin = jnp.concatenate([sin, -sin], axis=0).T * scale
        dk = total[:, :hd]
        swapped = jnp.concatenate([dk[:, hh:], dk[:, :hh]], axis=1)
        key_grad = (dk * cos + swapped * sin).astype(BF16)
        value_grad = total[:, hd:].astype(BF16)
        kg_ref[rows, :] = key_grad
        vg_ref[rows, :] = value_grad
        both_ref[rows, :hd] = key_grad
        both_ref[rows, hd:] = value_grad


def project_kernel(others, slots, r_ref, qg, kg, vg, qo, kvo, wq, wk, wv, *rest):
    j = pl.program_id(0)
    pieces, (out_ref, buf, sem) = rest[:8], rest[8:]
    qw, kw = qg.shape[1], kg.shape[1]

    def copy(i):
        return pltpu.make_async_copy(pieces[i], buf.at[i % slots], sem.at[i])

    for i in range(8):
        @pl.when(j == max(0, i - slots + 1))
        def _(i=i):
            copy(i).start()

    own = jnp.concatenate([wq[...], wk[...], wv[...]], axis=1)
    total = dot(jnp.concatenate([qg[...], kg[...], vg[...]], axis=1), own, NT)
    for i in range(8):
        @pl.when(j == i)
        def _(i=i):
            copy(i).wait()

    slot = lax.rem(j, slots)
    width = qw + 2 * kw
    for s in range(others):
        grads = jnp.concatenate(
            [qo[:, s * qw : (s + 1) * qw], kvo[:, s * 2 * kw : (s + 1) * 2 * kw]], axis=1
        )
        total = total + dot(grads, buf[slot, :, s * width : (s + 1) * width], NT)
    out_ref[...] = total.astype(BF16)


def prep_kernel(r_ref, k, v, q0, k0, v0, q1, k1, v1, kv, near, later):
    hd = k.shape[1]
    qw = q0.shape[1]
    kv[:, :hd] = k[...]
    kv[:, hd:] = v[...]
    for out, (a, b, c) in ((near, (q0, k0, v0)), (later, (q1, k1, v1))):
        out[:, :qw] = a[...]
        out[:, qw : qw + hd] = b[...]
        out[:, qw + hd :] = c[...]


def whole(shape):
    return pl.BlockSpec(shape, lambda *_: (0,) * len(shape))


def tie_kernel(*refs):
    pass


def tie(arrays, after):
    hbm = pl.BlockSpec(memory_space=pltpu.HBM)
    return pl.pallas_call(
        tie_kernel,
        out_shape=tuple(jax.ShapeDtypeStruct(x.shape, x.dtype) for x in arrays),
        in_specs=[hbm] * (len(arrays) + 1),
        out_specs=(hbm,) * len(arrays),
        input_output_aliases={i: i for i in range(len(arrays))},
        compiler_params=params(),
        name="tie",
    )(*arrays, after)


def params(**kw):
    return pltpu.CompilerParams(vmem_limit_bytes=VMEM_LIMIT, **kw)


def local(
    q_rot, k_rot, values, attn_out, out_grad, log_norm, stretch_ids, q_weight, k_weight, v_weight
):
    seq_count = lax.axis_size("seq")
    head_axis = lax.axis_size("head")
    tok, col_width = q_rot.shape
    hd = k_rot.shape[1]
    heads = col_width // hd
    half = tok // 2
    d_model = q_weight.shape[0]
    me = lax.axis_index("seq")
    my_head = lax.axis_index("head")
    eighth = d_model // 8
    part = lax.rem(me, 8)

    def shift_seq(x, by):
        return lax.ppermute(x, "seq", [(i, (i + by) % seq_count) for i in range(seq_count)])

    def swap_seq(x, bit):
        return lax.ppermute(x, "seq", [(i, i ^ bit) for i in range(seq_count)])

    def from_head(x, by):
        return lax.ppermute(x, "head", [(i, (i - by) % head_axis) for i in range(head_axis)])

    spot = jnp.stack([part, my_head])
    wblock = lambda w, flip: pl.BlockSpec((eighth, w.shape[1]), lambda i, r: (r[0] ^ flip, 0))
    weights = (q_weight, k_weight, v_weight)
    joined = jax.ShapeDtypeStruct((eighth, col_width + 2 * hd), BF16)
    kv, near, later = pl.pallas_call(
        prep_kernel,
        out_shape=(jax.ShapeDtypeStruct((tok, 2 * hd), BF16), joined, joined),
        grid_spec=pltpu.PrefetchScalarGridSpec(
            num_scalar_prefetch=1,
            grid=(1,),
            in_specs=[whole(k_rot.shape), whole(values.shape)]
            + [wblock(w, 0) for w in weights]
            + [wblock(w, 6) for w in weights],
            out_specs=(whole((tok, 2 * hd)), whole(joined.shape), whole(joined.shape)),
        ),
        compiler_params=params(),
        name="prep",
    )(spot, k_rot, values, *weights, *weights)

    def fetch(x):
        got = [from_head(x, s) for s in range(1, head_axis)]
        return got[0] if len(got) == 1 else jnp.concatenate(got, axis=1)

    near = fetch(near)
    kvs = [shift_seq(kv, stop) for stop in range(1, STOPS)]

    own_ids = lax.dynamic_index_in_dim(stretch_ids, me, 0, keepdims=False)
    offsets = jnp.arange(half, dtype=jnp.int32)
    positions = (own_ids[:, None] * half + offsets[None, :]).reshape(tok)
    tables = rotary_tables(positions, hd)

    smem = pl.BlockSpec(memory_space=pltpu.SMEM)
    hbm = pl.BlockSpec(memory_space=pltpu.HBM)
    unit = 10 * heads * half * half * hd
    dq0, kv0, norm, delta = pl.pallas_call(
        functools.partial(own_kernel, seq_count),
        out_shape=(
            jax.ShapeDtypeStruct((2, col_width, half), F32),
            jax.ShapeDtypeStruct((2, half, 2 * hd), F32),
            jax.ShapeDtypeStruct((2, heads, half), F32),
            jax.ShapeDtypeStruct((2, heads, half), F32),
        ),
        grid=(1,),
        in_specs=[smem]
        + [whole(x.shape) for x in (q_rot, k_rot, values, attn_out, out_grad, log_norm)],
        out_specs=(
            whole((2, col_width, half)),
            whole((2, half, 2 * hd)),
            whole((2, heads, half)),
            whole((2, heads, half)),
        ),
        compiler_params=params(),
        cost_estimate=pl.CostEstimate(
            flops=3 * unit, bytes_accessed=5 * 2**20, transcendentals=3 * heads * half * half
        ),
        name="own_stop",
    )(stretch_ids, q_rot, k_rot, values, attn_out, out_grad, log_norm)

    near, later = tie((near, later), norm)
    over_x = swap_seq(near, 2)
    over_z = swap_seq(near, 4)
    over_y = fetch(later)
    near_twin = swap_seq(near, 1)

    query_grad, *homes = pl.pallas_call(
        functools.partial(far_kernel, seq_count),
        out_shape=(jax.ShapeDtypeStruct((tok, col_width), BF16),)
        + (jax.ShapeDtypeStruct((tok, 2 * hd), BF16),) * (STOPS - 1),
        grid=(1,),
        in_specs=[smem]
        + [whole(x.shape) for x in (q_rot, out_grad, norm, delta, dq0, tables, *kvs)],
        out_specs=(whole((tok, col_width)),) + (whole((tok, 2 * hd)),) * (STOPS - 1),
        scratch_shapes=[
            pltpu.VMEM((2, col_width, half), F32),
            pltpu.VMEM((STOPS - 1, 2, half, 2 * hd), F32),
        ],
        compiler_params=params(),
        cost_estimate=pl.CostEstimate(
            flops=4 * unit, bytes_accessed=6 * 2**20, transcendentals=4 * heads * half * half
        ),
        name="far_stops",
    )(stretch_ids, q_rot, out_grad, norm, delta, dq0, tables, *kvs)

    out_rows = tok // head_axis

    def rows_for(x, h):
        return lax.dynamic_slice_in_dim(x, lax.rem(h, head_axis) * out_rows, out_rows, 0)

    def exchange(x):
        got = [
            from_head(rows_for(x, my_head + head_axis - s), s) for s in range(1, head_axis)
        ]
        return got[0] if len(got) == 1 else jnp.concatenate(got, axis=1)

    q_other = exchange(query_grad)
    homes = [shift_seq(x, -(i + 1)) for i, x in enumerate(homes)]
    over_x, over_z, over_y = tie((over_x, over_z, over_y), homes[0])
    pieces = [near, over_x, over_z, over_y, near_twin]
    pieces += [swap_seq(x, 1) for x in (over_x, over_z, over_y)]
    key_grad, value_grad, both = pl.pallas_call(
        finish_kernel,
        out_shape=(jax.ShapeDtypeStruct((tok, hd), BF16),) * 2
        + (jax.ShapeDtypeStruct((tok, 2 * hd), BF16),),
        grid=(1,),
        in_specs=[whole(tables.shape), whole(kv0.shape), hbm]
        + [whole(x.shape) for x in homes],
        out_specs=(whole((tok, hd)), whole((tok, hd)), whole((tok, 2 * hd))),
        compiler_params=params(),
        name="finish_keys",
    )(tables, kv0, q_other, *homes)
    kv_other = exchange(both)

    others = head_axis - 1
    slots = 8 if others == 1 else 2
    full = lambda shape: pl.BlockSpec(shape, lambda j, r: (0, 0))
    mine = lambda shape: pl.BlockSpec(shape, lambda j, r: (r[1], 0))
    which = lambda j, r: r[0] ^ (2 * (j % 4) + j // 4)
    wspec = lambda cols: pl.BlockSpec((eighth, cols), lambda j, r: (which(j, r), 0))
    d_input = pl.pallas_call(
        functools.partial(project_kernel, others, slots),
        out_shape=jax.ShapeDtypeStruct((out_rows, d_model), BF16),
        grid_spec=pltpu.PrefetchScalarGridSpec(
            num_scalar_prefetch=1,
            grid=(8,),
            in_specs=[
                mine((out_rows, col_width)),
                mine((out_rows, hd)),
                mine((out_rows, hd)),
                full((out_rows, col_width * others)),
                full((out_rows, 2 * hd * others)),
                wspec(col_width),
                wspec(hd),
                wspec(hd),
            ]
            + [hbm] * 8,
            out_specs=pl.BlockSpec((out_rows, eighth), lambda j, r: (0, which(j, r))),
            scratch_shapes=[
                pltpu.VMEM((slots, eighth, (col_width + 2 * hd) * others), BF16),
                pltpu.SemaphoreType.DMA((8,)),
            ],
        ),
        compiler_params=params(),
        name="project",
    )(
        spot,
        query_grad,
        key_grad,
        value_grad,
        q_other,
        kv_other,
        q_weight,
        k_weight,
        v_weight,
        *pieces,
    )
    return (d_input, key_grad, value_grad)


def solution(mesh):
    in_specs = (
        P("seq", "head"),
        P("seq", "head"),
        P("seq", "head"),
        P("seq", "head"),
        P("seq", "head"),
        P("head", "seq"),
        P(),
        P(None, "head"),
        P(None, "head"),
        P(None, "head"),
    )
    out_specs = (P(("seq", "head"), None), P("seq", "head"), P("seq", "head"))
    return jax.shard_map(local, mesh=mesh, in_specs=in_specs, out_specs=out_specs, check_vma=False)
```

```python
import functools
import math

import jax
import jax.numpy as jnp
from jax import lax
from jax.experimental import pallas as pl
from jax.experimental.pallas import tpu as pltpu
from jax.sharding import PartitionSpec as P

STOPS = 3
LOG2E = math.log2(math.e)
F32 = jnp.float32
BF16 = jnp.bfloat16
NT = (((1,), (1,)), ((), ()))
NN = (((1,), (0,)), ((), ()))
VMEM_LIMIT = 127 * 512 * 1024


def dot(a, b, dims):
    return lax.dot_general(a, b, dims, preferred_element_type=F32)


def rotary_tables(positions, head_dim):
    half_dim = head_dim // 2
    inverse = jnp.exp(
        jnp.arange(half_dim, dtype=F32) * (-2.0 * math.log(500000.0) / head_dim)
    )
    angles = inverse[:, None] * positions.astype(F32)[None, :]
    return jnp.stack([jnp.cos(angles), jnp.sin(angles)])


def lo_half(ids_ref, row):
    first, second = ids_ref[row, 0], ids_ref[row, 1]
    swap = (second < first).astype(jnp.int32)
    return swap, jnp.minimum(first, second)


def attend(q_ref, do_ref, norm_ref, delta_ref, dq_ref, kv_block, k_acc, q_half, k_half, masked):
    half = norm_ref.shape[2]
    heads = norm_ref.shape[1]
    keys, vals = kv_block(k_half)
    hd = keys.shape[1]
    scale = LOG2E / math.sqrt(hd)
    keys_t = keys.T
    rows = pl.ds(pl.multiple_of(q_half * half, half), half)
    dk = jnp.zeros((half, hd), F32)
    dv = jnp.zeros((half, hd), F32)
    if masked:
        visible = lax.broadcasted_iota(jnp.int32, (half, half), 0) <= lax.broadcasted_iota(
            jnp.int32, (half, half), 1
        )
    for h in range(heads):
        cols = slice(h * hd, (h + 1) * hd)
        q = q_ref[rows, cols]
        do = do_ref[rows, cols]
        probs = jnp.exp2(dot(keys, q, NT) * scale - norm_ref[q_half, h : h + 1, :])
        if masked:
            probs = jnp.where(visible, probs, 0.0)
        ds = (probs * (dot(vals, do, NT) - delta_ref[q_half, h : h + 1, :])).astype(BF16)
        dv = dv + dot(probs.astype(BF16), do, NN)
        dk = dk + dot(ds, q, NN)
        dq_ref[q_half, cols, :] += dot(keys_t, ds, NN)
    k_acc[k_half, :, :hd] += dk
    k_acc[k_half, :, hd:] += dv


def own_kernel(seq_count, ids_ref, q_ref, k_ref, v_ref, o_ref, do_ref, ln_ref, dq_ref, kv_ref, norm_ref, delta_ref):
    me = lax.axis_index("seq")
    heads, half = norm_ref.shape[1:]
    hd = k_ref.shape[1]
    for h in range(heads):
        cols = slice(h * hd, (h + 1) * hd)
        prod = do_ref[:, cols].astype(F32) * o_ref[:, cols].astype(F32)
        delta = jnp.sum(prod.T, axis=0, keepdims=True)
        for a in range(2):
            delta_ref[a, h : h + 1, :] = delta[:, a * half : (a + 1) * half]
    for a in range(2):
        norm_ref[a] = ln_ref[:, a * half : (a + 1) * half] * LOG2E
    dq_ref[...] = jnp.zeros_like(dq_ref)
    kv_ref[...] = jnp.zeros_like(kv_ref)

    def kv_block(b):
        rows = pl.ds(pl.multiple_of(b * half, half), half)
        return k_ref[rows, :], v_ref[rows, :]

    run = functools.partial(attend, q_ref, do_ref, norm_ref, delta_ref, dq_ref, kv_block, kv_ref)
    run(0, 0, True)
    run(1, 1, True)
    lo, _ = lo_half(ids_ref, me)
    run(1 - lo, lo, False)


def far_kernel(seq_count, ids_ref, q_ref, do_ref, norm_ref, delta_ref, dq0_ref, tab_ref, *rest):
    stops = STOPS - 1
    kv_refs, qg_ref, home_refs = rest[:stops], rest[stops], rest[stops + 1 : 2 * stops + 1]
    dq_ref, acc_ref = rest[2 * stops + 1 :]
    me = lax.axis_index("seq")
    heads, half = norm_ref.shape[1:]
    hd = kv_refs[0].shape[1] // 2
    dq_ref[...] = dq0_ref[...]
    lo, low_id = lo_half(ids_ref, me)
    for i in range(stops):
        kv_ref, acc = kv_refs[i], acc_ref.at[i]
        acc[...] = jnp.zeros_like(acc)
        row = lax.rem(me - (i + 1) + seq_count, seq_count)
        k_lo, k_low_id = lo_half(ids_ref, row)

        def kv_block(b, kv_ref=kv_ref):
            rows = pl.ds(pl.multiple_of(b * half, half), half)
            return kv_ref[rows, :hd], kv_ref[rows, hd:]

        run = functools.partial(attend, q_ref, do_ref, norm_ref, delta_ref, dq_ref, kv_block, acc)
        run(1 - lo, k_lo, False)
        lows = k_low_id < low_id
        run(jnp.where(lows, lo, 1 - lo), jnp.where(lows, k_lo, 1 - k_lo), False)
        for b in range(2):
            home_refs[i][b * half : (b + 1) * half, :] = acc[b].astype(BF16)
    scale = 1.0 / math.sqrt(hd)
    hh = hd // 2
    for a in range(2):
        cos = tab_ref[0, :, a * half : (a + 1) * half] * scale
        sin = tab_ref[1, :, a * half : (a + 1) * half] * scale
        for h in range(heads):
            first = dq_ref[a, h * hd : h * hd + hh, :]
            second = dq_ref[a, h * hd + hh : (h + 1) * hd, :]
            turned = jnp.concatenate(
                [first * cos + second * sin, second * cos - first * sin], axis=0
            )
            qg_ref[a * half : (a + 1) * half, h * hd : (h + 1) * hd] = turned.T.astype(BF16)


def finish_kernel(tab_ref, kv0_ref, *rest):
    home_refs, (kg_ref, vg_ref, both_ref) = rest[:-3], rest[-3:]
    half = kv0_ref.shape[1]
    hd = kg_ref.shape[1]
    hh = hd // 2
    scale = 1.0 / math.sqrt(hd)
    for a in range(2):
        rows = slice(a * half, (a + 1) * half)
        total = kv0_ref[a]
        for ref in home_refs:
            total = total + ref[rows, :].astype(F32)
        cos = tab_ref[0, :, rows]
        sin = tab_ref[1, :, rows]
        cos = jnp.concatenate([cos, cos], axis=0).T * scale
        sin = jnp.concatenate([sin, -sin], axis=0).T * scale
        dk = total[:, :hd]
        swapped = jnp.concatenate([dk[:, hh:], dk[:, :hh]], axis=1)
        key_grad = (dk * cos + swapped * sin).astype(BF16)
        value_grad = total[:, hd:].astype(BF16)
        kg_ref[rows, :] = key_grad
        vg_ref[rows, :] = value_grad
        both_ref[rows, :hd] = key_grad
        both_ref[rows, hd:] = value_grad


def own_project_kernel(r_ref, qg, wq, out_ref):
    out_ref[...] = dot(qg[...], wq[...], NT)


def project_kernel(others, slots, r_ref, partial, kg, vg, qo, kvo, wk, wv, *rest):
    j = pl.program_id(0)
    pieces, (out_ref, buf, sem) = rest[:8], rest[8:]
    kw = kg.shape[1]
    qw = qo.shape[1] // others
    eighth = pieces[0].shape[0]
    odd = lax.rem(r_ref[0], 2)

    def copies(i):
        for twin in range(2):
            place = pl.multiple_of((odd ^ twin) * eighth, eighth)
            yield pltpu.make_async_copy(
                pieces[2 * i + twin],
                buf.at[i % slots, pl.ds(place, eighth), :],
                sem.at[2 * i + twin],
            )

    for i in range(4):
        @pl.when(j == max(0, i - slots + 1))
        def _(i=i):
            for copy in copies(i):
                copy.start()

    total = partial[...] + dot(kg[...], wk[...], NT) + dot(vg[...], wv[...], NT)
    for i in range(4):
        @pl.when(j == i)
        def _(i=i):
            for copy in copies(i):
                copy.wait()

    slot = lax.rem(j, slots)
    width = qw + 2 * kw
    for s in range(others):
        total = total + dot(
            qo[:, s * qw : (s + 1) * qw], buf[slot, :, s * width : s * width + qw], NT
        )
        total = total + dot(
            kvo[:, s * 2 * kw : (s + 1) * 2 * kw],
            buf[slot, :, s * width + qw : (s + 1) * width],
            NT,
        )
    out_ref[...] = total.astype(BF16)


def prep_kernel(r_ref, k, v, q0, k0, v0, q1, k1, v1, kv, near, later):
    hd = k.shape[1]
    qw = q0.shape[1]
    kv[:, :hd] = k[...]
    kv[:, hd:] = v[...]
    for out, (a, b, c) in ((near, (q0, k0, v0)), (later, (q1, k1, v1))):
        out[:, :qw] = a[...]
        out[:, qw : qw + hd] = b[...]
        out[:, qw + hd :] = c[...]


def whole(shape):
    return pl.BlockSpec(shape, lambda *_: (0,) * len(shape))


def tie_kernel(*refs):
    pass


def tie(arrays, *after):
    hbm = pl.BlockSpec(memory_space=pltpu.HBM)
    return pl.pallas_call(
        tie_kernel,
        out_shape=tuple(jax.ShapeDtypeStruct(x.shape, x.dtype) for x in arrays),
        in_specs=[hbm] * (len(arrays) + len(after)),
        out_specs=(hbm,) * len(arrays),
        input_output_aliases={i: i for i in range(len(arrays))},
        compiler_params=params(),
        name="tie",
    )(*arrays, *after)


def params(**kw):
    return pltpu.CompilerParams(vmem_limit_bytes=VMEM_LIMIT, **kw)


def local(
    q_rot, k_rot, values, attn_out, out_grad, log_norm, stretch_ids, q_weight, k_weight, v_weight
):
    seq_count = lax.axis_size("seq")
    head_axis = lax.axis_size("head")
    tok, col_width = q_rot.shape
    hd = k_rot.shape[1]
    heads = col_width // hd
    half = tok // 2
    d_model = q_weight.shape[0]
    me = lax.axis_index("seq")
    my_head = lax.axis_index("head")
    eighth = d_model // 8
    part = lax.rem(me, 8)

    def shift_seq(x, by):
        return lax.ppermute(x, "seq", [(i, (i + by) % seq_count) for i in range(seq_count)])

    def swap_seq(x, bit):
        return lax.ppermute(x, "seq", [(i, i ^ bit) for i in range(seq_count)])

    def from_head(x, by):
        return lax.ppermute(x, "head", [(i, (i - by) % head_axis) for i in range(head_axis)])

    spot = jnp.stack([part, my_head])
    wblock = lambda w, flip: pl.BlockSpec((eighth, w.shape[1]), lambda i, r: (r[0] ^ flip, 0))
    weights = (q_weight, k_weight, v_weight)
    joined = jax.ShapeDtypeStruct((eighth, col_width + 2 * hd), BF16)
    kv, near, later = pl.pallas_call(
        prep_kernel,
        out_shape=(jax.ShapeDtypeStruct((tok, 2 * hd), BF16), joined, joined),
        grid_spec=pltpu.PrefetchScalarGridSpec(
            num_scalar_prefetch=1,
            grid=(1,),
            in_specs=[whole(k_rot.shape), whole(values.shape)]
            + [wblock(w, 0) for w in weights]
            + [wblock(w, 6) for w in weights],
            out_specs=(whole((tok, 2 * hd)), whole(joined.shape), whole(joined.shape)),
        ),
        compiler_params=params(),
        name="prep",
    )(spot, k_rot, values, *weights, *weights)

    def fetch(x):
        got = [from_head(x, s) for s in range(1, head_axis)]
        return got[0] if len(got) == 1 else jnp.concatenate(got, axis=1)

    near = fetch(near)
    kvs = [shift_seq(kv, stop) for stop in range(1, STOPS)]

    own_ids = lax.dynamic_index_in_dim(stretch_ids, me, 0, keepdims=False)
    offsets = jnp.arange(half, dtype=jnp.int32)
    positions = (own_ids[:, None] * half + offsets[None, :]).reshape(tok)
    tables = rotary_tables(positions, hd)

    smem = pl.BlockSpec(memory_space=pltpu.SMEM)
    hbm = pl.BlockSpec(memory_space=pltpu.HBM)
    unit = 10 * heads * half * half * hd
    dq0, kv0, norm, delta = pl.pallas_call(
        functools.partial(own_kernel, seq_count),
        out_shape=(
            jax.ShapeDtypeStruct((2, col_width, half), F32),
            jax.ShapeDtypeStruct((2, half, 2 * hd), F32),
            jax.ShapeDtypeStruct((2, heads, half), F32),
            jax.ShapeDtypeStruct((2, heads, half), F32),
        ),
        grid=(1,),
        in_specs=[smem]
        + [whole(x.shape) for x in (q_rot, k_rot, values, attn_out, out_grad, log_norm)],
        out_specs=(
            whole((2, col_width, half)),
            whole((2, half, 2 * hd)),
            whole((2, heads, half)),
            whole((2, heads, half)),
        ),
        compiler_params=params(),
        cost_estimate=pl.CostEstimate(
            flops=3 * unit, bytes_accessed=5 * 2**20, transcendentals=3 * heads * half * half
        ),
        name="own_stop",
    )(stretch_ids, q_rot, k_rot, values, attn_out, out_grad, log_norm)

    near, later = tie((near, later), norm)
    over_x = swap_seq(near, 2)
    over_z = swap_seq(near, 4)
    over_y = fetch(later)
    near_twin = swap_seq(near, 1)

    query_grad, *homes = pl.pallas_call(
        functools.partial(far_kernel, seq_count),
        out_shape=(jax.ShapeDtypeStruct((tok, col_width), BF16),)
        + (jax.ShapeDtypeStruct((tok, 2 * hd), BF16),) * (STOPS - 1),
        grid=(1,),
        in_specs=[smem]
        + [whole(x.shape) for x in (q_rot, out_grad, norm, delta, dq0, tables, *kvs)],
        out_specs=(whole((tok, col_width)),) + (whole((tok, 2 * hd)),) * (STOPS - 1),
        scratch_shapes=[
            pltpu.VMEM((2, col_width, half), F32),
            pltpu.VMEM((STOPS - 1, 2, half, 2 * hd), F32),
        ],
        compiler_params=params(),
        cost_estimate=pl.CostEstimate(
            flops=4 * unit, bytes_accessed=6 * 2**20, transcendentals=4 * heads * half * half
        ),
        name="far_stops",
    )(stretch_ids, q_rot, out_grad, norm, delta, dq0, tables, *kvs)

    out_rows = tok // head_axis

    def rows_for(x, h):
        return lax.dynamic_slice_in_dim(x, lax.rem(h, head_axis) * out_rows, out_rows, 0)

    def exchange(x):
        got = [
            from_head(rows_for(x, my_head + head_axis - s), s) for s in range(1, head_axis)
        ]
        return got[0] if len(got) == 1 else jnp.concatenate(got, axis=1)

    q_other = exchange(query_grad)
    quarter = 2 * eighth
    wquarter = lambda cols: pl.BlockSpec((quarter, cols), lambda j, r: ((r[0] // 2) ^ j, 0))
    column = pl.BlockSpec((out_rows, quarter), lambda j, r: (0, (r[0] // 2) ^ j))
    mine = lambda shape: pl.BlockSpec(shape, lambda j, r: (r[1], 0))
    partial = pl.pallas_call(
        own_project_kernel,
        out_shape=jax.ShapeDtypeStruct((out_rows, d_model), F32),
        grid_spec=pltpu.PrefetchScalarGridSpec(
            num_scalar_prefetch=1,
            grid=(4,),
            in_specs=[mine((out_rows, col_width)), wquarter(col_width)],
            out_specs=column,
        ),
        compiler_params=params(),
        cost_estimate=pl.CostEstimate(
            flops=2 * out_rows * d_model * col_width, bytes_accessed=11 * 2**20, transcendentals=0
        ),
        name="own_project",
    )(spot, query_grad, q_weight)
    homes = [shift_seq(x, -(i + 1)) for i, x in enumerate(homes)]
    over_x, over_z, over_y = tie((over_x, over_z, over_y), partial, q_other, *homes)
    pieces = [near, near_twin]
    for x in (over_x, over_z, over_y):
        pieces += [x, swap_seq(x, 1)]
    key_grad, value_grad, both = pl.pallas_call(
        finish_kernel,
        out_shape=(jax.ShapeDtypeStruct((tok, hd), BF16),) * 2
        + (jax.ShapeDtypeStruct((tok, 2 * hd), BF16),),
        grid=(1,),
        in_specs=[whole(tables.shape), whole(kv0.shape)]
        + [whole(x.shape) for x in homes],
        out_specs=(whole((tok, hd)), whole((tok, hd)), whole((tok, 2 * hd))),
        compiler_params=params(),
        name="finish_keys",
    )(tables, kv0, *homes)
    kv_other = exchange(both)

    others = head_axis - 1
    slots = 4 if others == 1 else 2
    full = lambda shape: pl.BlockSpec(shape, lambda j, r: (0, 0))
    mine = lambda shape: pl.BlockSpec(shape, lambda j, r: (r[1], 0))
    d_input = pl.pallas_call(
        functools.partial(project_kernel, others, slots),
        out_shape=jax.ShapeDtypeStruct((out_rows, d_model), BF16),
        grid_spec=pltpu.PrefetchScalarGridSpec(
            num_scalar_prefetch=1,
            grid=(4,),
            in_specs=[
                column,
                mine((out_rows, hd)),
                mine((out_rows, hd)),
                full((out_rows, col_width * others)),
                full((out_rows, 2 * hd * others)),
                wquarter(hd),
                wquarter(hd),
            ]
            + [hbm] * 8,
            out_specs=column,
            scratch_shapes=[
                pltpu.VMEM((slots, quarter, (col_width + 2 * hd) * others), BF16),
                pltpu.SemaphoreType.DMA((8,)),
            ],
        ),
        compiler_params=params(),
        name="project",
    )(
        spot,
        partial,
        key_grad,
        value_grad,
        q_other,
        kv_other,
        k_weight,
        v_weight,
        *pieces,
    )
    return (d_input, key_grad, value_grad)


def solution(mesh):
    in_specs = (
        P("seq", "head"),
        P("seq", "head"),
        P("seq", "head"),
        P("seq", "head"),
        P("seq", "head"),
        P("head", "seq"),
        P(),
        P(None, "head"),
        P(None, "head"),
        P(None, "head"),
    )
    out_specs = (P(("seq", "head"), None), P("seq", "head"), P("seq", "head"))
    return jax.shard_map(local, mesh=mesh, in_specs=in_specs, out_specs=out_specs, check_vma=False)
```

```python
import functools
import math

import jax
import jax.numpy as jnp
from jax import lax
from jax.experimental import pallas as pl
from jax.experimental.pallas import tpu as pltpu
from jax.sharding import PartitionSpec as P

STOPS = 3
LOG2E = math.log2(math.e)
F32 = jnp.float32
BF16 = jnp.bfloat16
NT = (((1,), (1,)), ((), ()))
NN = (((1,), (0,)), ((), ()))
VMEM_LIMIT = 127 * 512 * 1024


def dot(a, b, dims):
    return lax.dot_general(a, b, dims, preferred_element_type=F32)


def rotary_tables(positions, head_dim):
    half_dim = head_dim // 2
    inverse = jnp.exp(
        jnp.arange(half_dim, dtype=F32) * (-2.0 * math.log(500000.0) / head_dim)
    )
    angles = inverse[:, None] * positions.astype(F32)[None, :]
    return jnp.stack([jnp.cos(angles), jnp.sin(angles)])


def lo_half(ids_ref, row):
    first, second = ids_ref[row, 0], ids_ref[row, 1]
    swap = (second < first).astype(jnp.int32)
    return swap, jnp.minimum(first, second)


def attend(q_ref, do_ref, norm_ref, delta_ref, dq_ref, kv_block, k_acc, q_half, k_half, masked):
    half = norm_ref.shape[2]
    heads = norm_ref.shape[1]
    keys, vals = kv_block(k_half)
    hd = keys.shape[1]
    scale = LOG2E / math.sqrt(hd)
    keys_t = keys.T
    rows = pl.ds(pl.multiple_of(q_half * half, half), half)
    dk = jnp.zeros((half, hd), F32)
    dv = jnp.zeros((half, hd), F32)
    if masked:
        visible = lax.broadcasted_iota(jnp.int32, (half, half), 0) <= lax.broadcasted_iota(
            jnp.int32, (half, half), 1
        )
    for h in range(heads):
        cols = slice(h * hd, (h + 1) * hd)
        q = q_ref[rows, cols]
        do = do_ref[rows, cols]
        probs = jnp.exp2(dot(keys, q, NT) * scale - norm_ref[q_half, h : h + 1, :])
        if masked:
            probs = jnp.where(visible, probs, 0.0)
        ds = (probs * (dot(vals, do, NT) - delta_ref[q_half, h : h + 1, :])).astype(BF16)
        dv = dv + dot(probs.astype(BF16), do, NN)
        dk = dk + dot(ds, q, NN)
        dq_ref[q_half, cols, :] += dot(keys_t, ds, NN)
    k_acc[k_half, :, :hd] += dk
    k_acc[k_half, :, hd:] += dv


def own_kernel(seq_count, ids_ref, q_ref, k_ref, v_ref, o_ref, do_ref, ln_ref, dq_ref, kv_ref, norm_ref, delta_ref):
    me = lax.axis_index("seq")
    heads, half = norm_ref.shape[1:]
    hd = k_ref.shape[1]
    for h in range(heads):
        cols = slice(h * hd, (h + 1) * hd)
        prod = do_ref[:, cols].astype(F32) * o_ref[:, cols].astype(F32)
        delta = jnp.sum(prod.T, axis=0, keepdims=True)
        for a in range(2):
            delta_ref[a, h : h + 1, :] = delta[:, a * half : (a + 1) * half]
    for a in range(2):
        norm_ref[a] = ln_ref[:, a * half : (a + 1) * half] * LOG2E
    dq_ref[...] = jnp.zeros_like(dq_ref)
    kv_ref[...] = jnp.zeros_like(kv_ref)

    def kv_block(b):
        rows = pl.ds(pl.multiple_of(b * half, half), half)
        return k_ref[rows, :], v_ref[rows, :]

    run = functools.partial(attend, q_ref, do_ref, norm_ref, delta_ref, dq_ref, kv_block, kv_ref)
    run(0, 0, True)
    run(1, 1, True)
    lo, _ = lo_half(ids_ref, me)
    run(1 - lo, lo, False)


def far_kernel(seq_count, ids_ref, q_ref, do_ref, norm_ref, delta_ref, dq0_ref, tab_ref, *rest):
    stops = STOPS - 1
    kv_refs, qg_ref, home_refs = rest[:stops], rest[stops], rest[stops + 1 : 2 * stops + 1]
    dq_ref, acc_ref = rest[2 * stops + 1 :]
    me = lax.axis_index("seq")
    heads, half = norm_ref.shape[1:]
    hd = kv_refs[0].shape[1] // 2
    dq_ref[...] = dq0_ref[...]
    lo, low_id = lo_half(ids_ref, me)
    for i in range(stops):
        kv_ref, acc = kv_refs[i], acc_ref.at[i]
        acc[...] = jnp.zeros_like(acc)
        row = lax.rem(me - (i + 1) + seq_count, seq_count)
        k_lo, k_low_id = lo_half(ids_ref, row)

        def kv_block(b, kv_ref=kv_ref):
            rows = pl.ds(pl.multiple_of(b * half, half), half)
            return kv_ref[rows, :hd], kv_ref[rows, hd:]

        run = functools.partial(attend, q_ref, do_ref, norm_ref, delta_ref, dq_ref, kv_block, acc)
        run(1 - lo, k_lo, False)
        lows = k_low_id < low_id
        run(jnp.where(lows, lo, 1 - lo), jnp.where(lows, k_lo, 1 - k_lo), False)
        for b in range(2):
            home_refs[i][b * half : (b + 1) * half, :] = acc[b].astype(BF16)
    scale = 1.0 / math.sqrt(hd)
    hh = hd // 2
    for a in range(2):
        cos = tab_ref[0, :, a * half : (a + 1) * half] * scale
        sin = tab_ref[1, :, a * half : (a + 1) * half] * scale
        for h in range(heads):
            first = dq_ref[a, h * hd : h * hd + hh, :]
            second = dq_ref[a, h * hd + hh : (h + 1) * hd, :]
            turned = jnp.concatenate(
                [first * cos + second * sin, second * cos - first * sin], axis=0
            )
            qg_ref[a * half : (a + 1) * half, h * hd : (h + 1) * hd] = turned.T.astype(BF16)


def finish_kernel(tab_ref, kv0_ref, *rest):
    home_refs, (kg_ref, vg_ref, both_ref) = rest[:-3], rest[-3:]
    half = kv0_ref.shape[1]
    hd = kg_ref.shape[1]
    hh = hd // 2
    scale = 1.0 / math.sqrt(hd)
    for a in range(2):
        rows = slice(a * half, (a + 1) * half)
        total = kv0_ref[a]
        for ref in home_refs:
            total = total + ref[rows, :].astype(F32)
        cos = tab_ref[0, :, rows]
        sin = tab_ref[1, :, rows]
        cos = jnp.concatenate([cos, cos], axis=0).T * scale
        sin = jnp.concatenate([sin, -sin], axis=0).T * scale
        dk = total[:, :hd]
        swapped = jnp.concatenate([dk[:, hh:], dk[:, :hh]], axis=1)
        key_grad = (dk * cos + swapped * sin).astype(BF16)
        value_grad = total[:, hd:].astype(BF16)
        kg_ref[rows, :] = key_grad
        vg_ref[rows, :] = value_grad
        both_ref[rows, :hd] = key_grad
        both_ref[rows, hd:] = value_grad


def project_kernel(others, slots, r_ref, qg, kg, vg, qo, kvo, wq, wk, wv, *rest):
    j = pl.program_id(0)
    pieces, (out_ref, buf, sem) = rest[:8], rest[8:]
    kw = kg.shape[1]
    qw = qo.shape[1] // others
    eighth = pieces[0].shape[0]
    odd = lax.rem(r_ref[0], 2)

    def copies(i):
        for twin in range(2):
            place = pl.multiple_of((odd ^ twin) * eighth, eighth)
            yield pltpu.make_async_copy(
                pieces[2 * i + twin],
                buf.at[i % slots, pl.ds(place, eighth), :],
                sem.at[2 * i + twin],
            )

    for i in range(4):
        @pl.when(j == max(0, i - slots + 1))
        def _(i=i):
            for copy in copies(i):
                copy.start()

    total = dot(qg[...], wq[...], NT) + dot(kg[...], wk[...], NT) + dot(vg[...], wv[...], NT)
    for i in range(4):
        @pl.when(j == i)
        def _(i=i):
            for copy in copies(i):
                copy.wait()

    slot = lax.rem(j, slots)
    width = qw + 2 * kw
    for s in range(others):
        total = total + dot(
            qo[:, s * qw : (s + 1) * qw], buf[slot, :, s * width : s * width + qw], NT
        )
        total = total + dot(
            kvo[:, s * 2 * kw : (s + 1) * 2 * kw],
            buf[slot, :, s * width + qw : (s + 1) * width],
            NT,
        )
    out_ref[...] = total.astype(BF16)


def prep_kernel(r_ref, k, v, q0, k0, v0, q1, k1, v1, kv, near, later):
    hd = k.shape[1]
    qw = q0.shape[1]
    kv[:, :hd] = k[...]
    kv[:, hd:] = v[...]
    for out, (a, b, c) in ((near, (q0, k0, v0)), (later, (q1, k1, v1))):
        out[:, :qw] = a[...]
        out[:, qw : qw + hd] = b[...]
        out[:, qw + hd :] = c[...]


def whole(shape):
    return pl.BlockSpec(shape, lambda *_: (0,) * len(shape))


def tie_kernel(*refs):
    pass


def tie(arrays, *after):
    hbm = pl.BlockSpec(memory_space=pltpu.HBM)
    return pl.pallas_call(
        tie_kernel,
        out_shape=tuple(jax.ShapeDtypeStruct(x.shape, x.dtype) for x in arrays),
        in_specs=[hbm] * (len(arrays) + len(after)),
        out_specs=(hbm,) * len(arrays),
        input_output_aliases={i: i for i in range(len(arrays))},
        compiler_params=params(),
        name="tie",
    )(*arrays, *after)


def params(**kw):
    return pltpu.CompilerParams(vmem_limit_bytes=VMEM_LIMIT, **kw)


def local(
    q_rot, k_rot, values, attn_out, out_grad, log_norm, stretch_ids, q_weight, k_weight, v_weight
):
    seq_count = lax.axis_size("seq")
    head_axis = lax.axis_size("head")
    tok, col_width = q_rot.shape
    hd = k_rot.shape[1]
    heads = col_width // hd
    half = tok // 2
    d_model = q_weight.shape[0]
    me = lax.axis_index("seq")
    my_head = lax.axis_index("head")
    eighth = d_model // 8
    part = lax.rem(me, 8)

    def shift_seq(x, by):
        return lax.ppermute(x, "seq", [(i, (i + by) % seq_count) for i in range(seq_count)])

    def swap_seq(x, bit):
        return lax.ppermute(x, "seq", [(i, i ^ bit) for i in range(seq_count)])

    def from_head(x, by):
        return lax.ppermute(x, "head", [(i, (i - by) % head_axis) for i in range(head_axis)])

    spot = jnp.stack([part, my_head])
    wblock = lambda w, flip: pl.BlockSpec((eighth, w.shape[1]), lambda i, r: (r[0] ^ flip, 0))
    weights = (q_weight, k_weight, v_weight)
    joined = jax.ShapeDtypeStruct((eighth, col_width + 2 * hd), BF16)
    kv, near, later = pl.pallas_call(
        prep_kernel,
        out_shape=(jax.ShapeDtypeStruct((tok, 2 * hd), BF16), joined, joined),
        grid_spec=pltpu.PrefetchScalarGridSpec(
            num_scalar_prefetch=1,
            grid=(1,),
            in_specs=[whole(k_rot.shape), whole(values.shape)]
            + [wblock(w, 0) for w in weights]
            + [wblock(w, 6) for w in weights],
            out_specs=(whole((tok, 2 * hd)), whole(joined.shape), whole(joined.shape)),
        ),
        compiler_params=params(),
        name="prep",
    )(spot, k_rot, values, *weights, *weights)

    def fetch(x):
        got = [from_head(x, s) for s in range(1, head_axis)]
        return got[0] if len(got) == 1 else jnp.concatenate(got, axis=1)

    near = fetch(near)
    kvs = [shift_seq(kv, stop) for stop in range(1, STOPS)]

    own_ids = lax.dynamic_index_in_dim(stretch_ids, me, 0, keepdims=False)
    offsets = jnp.arange(half, dtype=jnp.int32)
    positions = (own_ids[:, None] * half + offsets[None, :]).reshape(tok)
    tables = rotary_tables(positions, hd)

    smem = pl.BlockSpec(memory_space=pltpu.SMEM)
    hbm = pl.BlockSpec(memory_space=pltpu.HBM)
    unit = 10 * heads * half * half * hd
    dq0, kv0, norm, delta = pl.pallas_call(
        functools.partial(own_kernel, seq_count),
        out_shape=(
            jax.ShapeDtypeStruct((2, col_width, half), F32),
            jax.ShapeDtypeStruct((2, half, 2 * hd), F32),
            jax.ShapeDtypeStruct((2, heads, half), F32),
            jax.ShapeDtypeStruct((2, heads, half), F32),
        ),
        grid=(1,),
        in_specs=[smem]
        + [whole(x.shape) for x in (q_rot, k_rot, values, attn_out, out_grad, log_norm)],
        out_specs=(
            whole((2, col_width, half)),
            whole((2, half, 2 * hd)),
            whole((2, heads, half)),
            whole((2, heads, half)),
        ),
        compiler_params=params(),
        cost_estimate=pl.CostEstimate(
            flops=3 * unit, bytes_accessed=5 * 2**20, transcendentals=3 * heads * half * half
        ),
        name="own_stop",
    )(stretch_ids, q_rot, k_rot, values, attn_out, out_grad, log_norm)

    near, later, norm = tie((near, later, norm))
    over_x = swap_seq(near, 2)
    over_z = swap_seq(near, 4)
    over_y = fetch(later)

    query_grad, *homes = pl.pallas_call(
        functools.partial(far_kernel, seq_count),
        out_shape=(jax.ShapeDtypeStruct((tok, col_width), BF16),)
        + (jax.ShapeDtypeStruct((tok, 2 * hd), BF16),) * (STOPS - 1),
        grid=(1,),
        in_specs=[smem]
        + [whole(x.shape) for x in (q_rot, out_grad, norm, delta, dq0, tables, *kvs)],
        out_specs=(whole((tok, col_width)),) + (whole((tok, 2 * hd)),) * (STOPS - 1),
        scratch_shapes=[
            pltpu.VMEM((2, col_width, half), F32),
            pltpu.VMEM((STOPS - 1, 2, half, 2 * hd), F32),
        ],
        compiler_params=params(),
        cost_estimate=pl.CostEstimate(
            flops=4 * unit, bytes_accessed=6 * 2**20, transcendentals=4 * heads * half * half
        ),
        name="far_stops",
    )(stretch_ids, q_rot, out_grad, norm, delta, dq0, tables, *kvs)

    out_rows = tok // head_axis

    def rows_for(x, h):
        return lax.dynamic_slice_in_dim(x, lax.rem(h, head_axis) * out_rows, out_rows, 0)

    def exchange(x):
        got = [
            from_head(rows_for(x, my_head + head_axis - s), s) for s in range(1, head_axis)
        ]
        return got[0] if len(got) == 1 else jnp.concatenate(got, axis=1)

    q_other = exchange(query_grad)
    quarter = 2 * eighth
    wquarter = lambda cols: pl.BlockSpec((quarter, cols), lambda j, r: ((r[0] // 2) ^ j, 0))
    column = pl.BlockSpec((out_rows, quarter), lambda j, r: (0, (r[0] // 2) ^ j))
    mine = lambda shape: pl.BlockSpec(shape, lambda j, r: (r[1], 0))
    homes = [shift_seq(x, -(i + 1)) for i, x in enumerate(homes)]
    pieces = []
    for x in tie((near, over_x, over_z, over_y), q_other, *homes):
        pieces += [x, swap_seq(x, 1)]
    key_grad, value_grad, both = pl.pallas_call(
        finish_kernel,
        out_shape=(jax.ShapeDtypeStruct((tok, hd), BF16),) * 2
        + (jax.ShapeDtypeStruct((tok, 2 * hd), BF16),),
        grid=(1,),
        in_specs=[whole(tables.shape), whole(kv0.shape)]
        + [whole(x.shape) for x in homes],
        out_specs=(whole((tok, hd)), whole((tok, hd)), whole((tok, 2 * hd))),
        compiler_params=params(),
        name="finish_keys",
    )(tables, kv0, *homes)
    kv_other = exchange(both)

    others = head_axis - 1
    slots = 4 if others == 1 else 2
    full = lambda shape: pl.BlockSpec(shape, lambda j, r: (0, 0))
    mine = lambda shape: pl.BlockSpec(shape, lambda j, r: (r[1], 0))
    d_input = pl.pallas_call(
        functools.partial(project_kernel, others, slots),
        out_shape=jax.ShapeDtypeStruct((out_rows, d_model), BF16),
        grid_spec=pltpu.PrefetchScalarGridSpec(
            num_scalar_prefetch=1,
            grid=(4,),
            in_specs=[
                mine((out_rows, col_width)),
                mine((out_rows, hd)),
                mine((out_rows, hd)),
                full((out_rows, col_width * others)),
                full((out_rows, 2 * hd * others)),
                wquarter(col_width),
                wquarter(hd),
                wquarter(hd),
            ]
            + [hbm] * 8,
            out_specs=column,
            scratch_shapes=[
                pltpu.VMEM((slots, quarter, (col_width + 2 * hd) * others), BF16),
                pltpu.SemaphoreType.DMA((8,)),
            ],
        ),
        compiler_params=params(),
        name="project",
    )(
        spot,
        query_grad,
        key_grad,
        value_grad,
        q_other,
        kv_other,
        q_weight,
        k_weight,
        v_weight,
        *pieces,
    )
    return (d_input, key_grad, value_grad)


def solution(mesh):
    in_specs = (
        P("seq", "head"),
        P("seq", "head"),
        P("seq", "head"),
        P("seq", "head"),
        P("seq", "head"),
        P("head", "seq"),
        P(),
        P(None, "head"),
        P(None, "head"),
        P(None, "head"),
    )
    out_specs = (P(("seq", "head"), None), P("seq", "head"), P("seq", "head"))
    return jax.shard_map(local, mesh=mesh, in_specs=in_specs, out_specs=out_specs, check_vma=False)
```

```python
import functools
import math

import jax
import jax.numpy as jnp
from jax import lax
from jax.experimental import pallas as pl
from jax.experimental.pallas import tpu as pltpu
from jax.sharding import PartitionSpec as P

STOPS = 3
LOG2E = math.log2(math.e)
F32 = jnp.float32
BF16 = jnp.bfloat16
NT = (((1,), (1,)), ((), ()))
NN = (((1,), (0,)), ((), ()))
VMEM_LIMIT = 127 * 512 * 1024


def dot(a, b, dims):
    return lax.dot_general(a, b, dims, preferred_element_type=F32)


def rotary_tables(positions, head_dim):
    half_dim = head_dim // 2
    inverse = jnp.exp(
        jnp.arange(half_dim, dtype=F32) * (-2.0 * math.log(500000.0) / head_dim)
    )
    angles = inverse[:, None] * positions.astype(F32)[None, :]
    return jnp.stack([jnp.cos(angles), jnp.sin(angles)])


def lo_half(ids_ref, row):
    first, second = ids_ref[row, 0], ids_ref[row, 1]
    swap = (second < first).astype(jnp.int32)
    return swap, jnp.minimum(first, second)


def attend(q_ref, do_ref, norm_ref, delta_ref, dq_ref, kv_block, k_acc, q_half, k_half, masked):
    half = norm_ref.shape[2]
    heads = norm_ref.shape[1]
    keys, vals = kv_block(k_half)
    hd = keys.shape[1]
    scale = LOG2E / math.sqrt(hd)
    keys_t = keys.T
    rows = pl.ds(pl.multiple_of(q_half * half, half), half)
    dk = jnp.zeros((half, hd), F32)
    dv = jnp.zeros((half, hd), F32)
    if masked:
        visible = lax.broadcasted_iota(jnp.int32, (half, half), 0) <= lax.broadcasted_iota(
            jnp.int32, (half, half), 1
        )
    for h in range(heads):
        cols = slice(h * hd, (h + 1) * hd)
        q = q_ref[rows, cols]
        do = do_ref[rows, cols]
        probs = jnp.exp2(dot(keys, q, NT) * scale - norm_ref[q_half, h : h + 1, :])
        if masked:
            probs = jnp.where(visible, probs, 0.0)
        ds = (probs * (dot(vals, do, NT) - delta_ref[q_half, h : h + 1, :])).astype(BF16)
        dv = dv + dot(probs.astype(BF16), do, NN)
        dk = dk + dot(ds, q, NN)
        dq_ref[q_half, cols, :] += dot(keys_t, ds, NN)
    k_acc[k_half, :, :hd] += dk
    k_acc[k_half, :, hd:] += dv


def own_kernel(seq_count, ids_ref, q_ref, k_ref, v_ref, o_ref, do_ref, ln_ref, dq_ref, kv_ref, norm_ref, delta_ref):
    me = lax.axis_index("seq")
    heads, half = norm_ref.shape[1:]
    hd = k_ref.shape[1]
    for h in range(heads):
        cols = slice(h * hd, (h + 1) * hd)
        prod = do_ref[:, cols].astype(F32) * o_ref[:, cols].astype(F32)
        delta = jnp.sum(prod.T, axis=0, keepdims=True)
        for a in range(2):
            delta_ref[a, h : h + 1, :] = delta[:, a * half : (a + 1) * half]
    for a in range(2):
        norm_ref[a] = ln_ref[:, a * half : (a + 1) * half] * LOG2E
    dq_ref[...] = jnp.zeros_like(dq_ref)
    kv_ref[...] = jnp.zeros_like(kv_ref)

    def kv_block(b):
        rows = pl.ds(pl.multiple_of(b * half, half), half)
        return k_ref[rows, :], v_ref[rows, :]

    run = functools.partial(attend, q_ref, do_ref, norm_ref, delta_ref, dq_ref, kv_block, kv_ref)
    run(0, 0, True)
    run(1, 1, True)
    lo, _ = lo_half(ids_ref, me)
    run(1 - lo, lo, False)


def far_kernel(seq_count, ids_ref, q_ref, do_ref, norm_ref, delta_ref, dq0_ref, tab_ref, *rest):
    stops = STOPS - 1
    kv_refs, qg_ref, home_refs = rest[:stops], rest[stops], rest[stops + 1 : 2 * stops + 1]
    dq_ref, acc_ref = rest[2 * stops + 1 :]
    me = lax.axis_index("seq")
    heads, half = norm_ref.shape[1:]
    hd = kv_refs[0].shape[1] // 2
    dq_ref[...] = dq0_ref[...]
    lo, low_id = lo_half(ids_ref, me)
    for i in range(stops):
        kv_ref, acc = kv_refs[i], acc_ref.at[i]
        acc[...] = jnp.zeros_like(acc)
        row = lax.rem(me - (i + 1) + seq_count, seq_count)
        k_lo, k_low_id = lo_half(ids_ref, row)

        def kv_block(b, kv_ref=kv_ref):
            rows = pl.ds(pl.multiple_of(b * half, half), half)
            return kv_ref[rows, :hd], kv_ref[rows, hd:]

        run = functools.partial(attend, q_ref, do_ref, norm_ref, delta_ref, dq_ref, kv_block, acc)
        run(1 - lo, k_lo, False)
        lows = k_low_id < low_id
        run(jnp.where(lows, lo, 1 - lo), jnp.where(lows, k_lo, 1 - k_lo), False)
        for b in range(2):
            home_refs[i][b * half : (b + 1) * half, :] = acc[b].astype(BF16)
    scale = 1.0 / math.sqrt(hd)
    hh = hd // 2
    for a in range(2):
        cos = tab_ref[0, :, a * half : (a + 1) * half] * scale
        sin = tab_ref[1, :, a * half : (a + 1) * half] * scale
        for h in range(heads):
            first = dq_ref[a, h * hd : h * hd + hh, :]
            second = dq_ref[a, h * hd + hh : (h + 1) * hd, :]
            turned = jnp.concatenate(
                [first * cos + second * sin, second * cos - first * sin], axis=0
            )
            qg_ref[a * half : (a + 1) * half, h * hd : (h + 1) * hd] = turned.T.astype(BF16)


def finish_kernel(tab_ref, kv0_ref, after_ref, *rest):
    home_refs, (kg_ref, vg_ref, both_ref) = rest[:-3], rest[-3:]
    half = kv0_ref.shape[1]
    hd = kg_ref.shape[1]
    hh = hd // 2
    scale = 1.0 / math.sqrt(hd)
    for a in range(2):
        rows = slice(a * half, (a + 1) * half)
        total = kv0_ref[a]
        for ref in home_refs:
            total = total + ref[rows, :].astype(F32)
        cos = tab_ref[0, :, rows]
        sin = tab_ref[1, :, rows]
        cos = jnp.concatenate([cos, cos], axis=0).T * scale
        sin = jnp.concatenate([sin, -sin], axis=0).T * scale
        dk = total[:, :hd]
        swapped = jnp.concatenate([dk[:, hh:], dk[:, :hh]], axis=1)
        key_grad = (dk * cos + swapped * sin).astype(BF16)
        value_grad = total[:, hd:].astype(BF16)
        kg_ref[rows, :] = key_grad
        vg_ref[rows, :] = value_grad
        both_ref[rows, :hd] = key_grad
        both_ref[rows, hd:] = value_grad


def project_kernel(others, slots, r_ref, qg, kg, vg, qo, kvo, wq, wk, wv, *rest):
    j = pl.program_id(0)
    pieces, (out_ref, buf, sem) = rest[:8], rest[8:]
    qw, kw = qg.shape[1], kg.shape[1]

    def copy(i):
        return pltpu.make_async_copy(pieces[i], buf.at[i % slots], sem.at[i])

    for i in range(8):
        @pl.when(j == max(0, i - slots + 1))
        def _(i=i):
            copy(i).start()

    total = dot(qg[...], wq[...], NT) + dot(kg[...], wk[...], NT) + dot(vg[...], wv[...], NT)
    for i in range(8):
        @pl.when(j == i)
        def _(i=i):
            copy(i).wait()

    slot = lax.rem(j, slots)
    width = qw + 2 * kw
    for s in range(others):
        total = total + dot(
            qo[:, s * qw : (s + 1) * qw], buf[slot, :, s * width : s * width + qw], NT
        )
        total = total + dot(
            kvo[:, s * 2 * kw : (s + 1) * 2 * kw],
            buf[slot, :, s * width + qw : (s + 1) * width],
            NT,
        )
    out_ref[...] = total.astype(BF16)


def prep_kernel(r_ref, k, v, q0, k0, v0, q1, k1, v1, kv, near, later):
    hd = k.shape[1]
    qw = q0.shape[1]
    kv[:, :hd] = k[...]
    kv[:, hd:] = v[...]
    for out, (a, b, c) in ((near, (q0, k0, v0)), (later, (q1, k1, v1))):
        out[:, :qw] = a[...]
        out[:, qw : qw + hd] = b[...]
        out[:, qw + hd :] = c[...]


def whole(shape):
    return pl.BlockSpec(shape, lambda *_: (0,) * len(shape))


def tie_kernel(*refs):
    pass


def tie(arrays, after):
    hbm = pl.BlockSpec(memory_space=pltpu.HBM)
    return pl.pallas_call(
        tie_kernel,
        out_shape=tuple(jax.ShapeDtypeStruct(x.shape, x.dtype) for x in arrays),
        in_specs=[hbm] * (len(arrays) + 1),
        out_specs=(hbm,) * len(arrays),
        input_output_aliases={i: i for i in range(len(arrays))},
        compiler_params=params(),
        name="tie",
    )(*arrays, after)


def params(**kw):
    return pltpu.CompilerParams(vmem_limit_bytes=VMEM_LIMIT, **kw)


def local(
    q_rot, k_rot, values, attn_out, out_grad, log_norm, stretch_ids, q_weight, k_weight, v_weight
):
    seq_count = lax.axis_size("seq")
    head_axis = lax.axis_size("head")
    tok, col_width = q_rot.shape
    hd = k_rot.shape[1]
    heads = col_width // hd
    half = tok // 2
    d_model = q_weight.shape[0]
    me = lax.axis_index("seq")
    my_head = lax.axis_index("head")
    eighth = d_model // 8
    part = lax.rem(me, 8)

    def shift_seq(x, by):
        return lax.ppermute(x, "seq", [(i, (i + by) % seq_count) for i in range(seq_count)])

    def swap_seq(x, bit):
        return lax.ppermute(x, "seq", [(i, i ^ bit) for i in range(seq_count)])

    def from_head(x, by):
        return lax.ppermute(x, "head", [(i, (i - by) % head_axis) for i in range(head_axis)])

    spot = jnp.stack([part, my_head])
    wblock = lambda w, flip: pl.BlockSpec((eighth, w.shape[1]), lambda i, r: (r[0] ^ flip, 0))
    weights = (q_weight, k_weight, v_weight)
    joined = jax.ShapeDtypeStruct((eighth, col_width + 2 * hd), BF16)
    kv, near, later = pl.pallas_call(
        prep_kernel,
        out_shape=(jax.ShapeDtypeStruct((tok, 2 * hd), BF16), joined, joined),
        grid_spec=pltpu.PrefetchScalarGridSpec(
            num_scalar_prefetch=1,
            grid=(1,),
            in_specs=[whole(k_rot.shape), whole(values.shape)]
            + [wblock(w, 0) for w in weights]
            + [wblock(w, 6) for w in weights],
            out_specs=(whole((tok, 2 * hd)), whole(joined.shape), whole(joined.shape)),
        ),
        compiler_params=params(),
        name="prep",
    )(spot, k_rot, values, *weights, *weights)

    def fetch(x):
        got = [from_head(x, s) for s in range(1, head_axis)]
        return got[0] if len(got) == 1 else jnp.concatenate(got, axis=1)

    near = fetch(near)
    kvs = [shift_seq(kv, stop) for stop in range(1, STOPS)]

    own_ids = lax.dynamic_index_in_dim(stretch_ids, me, 0, keepdims=False)
    offsets = jnp.arange(half, dtype=jnp.int32)
    positions = (own_ids[:, None] * half + offsets[None, :]).reshape(tok)
    tables = rotary_tables(positions, hd)

    smem = pl.BlockSpec(memory_space=pltpu.SMEM)
    hbm = pl.BlockSpec(memory_space=pltpu.HBM)
    unit = 10 * heads * half * half * hd
    dq0, kv0, norm, delta = pl.pallas_call(
        functools.partial(own_kernel, seq_count),
        out_shape=(
            jax.ShapeDtypeStruct((2, col_width, half), F32),
            jax.ShapeDtypeStruct((2, half, 2 * hd), F32),
            jax.ShapeDtypeStruct((2, heads, half), F32),
            jax.ShapeDtypeStruct((2, heads, half), F32),
        ),
        grid=(1,),
        in_specs=[smem]
        + [whole(x.shape) for x in (q_rot, k_rot, values, attn_out, out_grad, log_norm)],
        out_specs=(
            whole((2, col_width, half)),
            whole((2, half, 2 * hd)),
            whole((2, heads, half)),
            whole((2, heads, half)),
        ),
        compiler_params=params(),
        cost_estimate=pl.CostEstimate(
            flops=3 * unit, bytes_accessed=5 * 2**20, transcendentals=3 * heads * half * half
        ),
        name="own_stop",
    )(stretch_ids, q_rot, k_rot, values, attn_out, out_grad, log_norm)

    near, later = tie((near, later), norm)
    over_x = swap_seq(near, 2)
    over_z = swap_seq(near, 4)
    over_y = fetch(later)
    near_twin = swap_seq(near, 1)

    query_grad, *homes = pl.pallas_call(
        functools.partial(far_kernel, seq_count),
        out_shape=(jax.ShapeDtypeStruct((tok, col_width), BF16),)
        + (jax.ShapeDtypeStruct((tok, 2 * hd), BF16),) * (STOPS - 1),
        grid=(1,),
        in_specs=[smem]
        + [whole(x.shape) for x in (q_rot, out_grad, norm, delta, dq0, tables, *kvs)],
        out_specs=(whole((tok, col_width)),) + (whole((tok, 2 * hd)),) * (STOPS - 1),
        scratch_shapes=[
            pltpu.VMEM((2, col_width, half), F32),
            pltpu.VMEM((STOPS - 1, 2, half, 2 * hd), F32),
        ],
        compiler_params=params(),
        cost_estimate=pl.CostEstimate(
            flops=4 * unit, bytes_accessed=6 * 2**20, transcendentals=4 * heads * half * half
        ),
        name="far_stops",
    )(stretch_ids, q_rot, out_grad, norm, delta, dq0, tables, *kvs)

    out_rows = tok // head_axis

    def rows_for(x, h):
        return lax.dynamic_slice_in_dim(x, lax.rem(h, head_axis) * out_rows, out_rows, 0)

    def exchange(x):
        got = [
            from_head(rows_for(x, my_head + head_axis - s), s) for s in range(1, head_axis)
        ]
        return got[0] if len(got) == 1 else jnp.concatenate(got, axis=1)

    q_other = exchange(query_grad)
    homes = [shift_seq(x, -(i + 1)) for i, x in enumerate(homes)]
    over_x, over_z, over_y = tie((over_x, over_z, over_y), homes[0])
    pieces = [near, over_x, over_z, over_y, near_twin]
    pieces += [swap_seq(x, 1) for x in (over_x, over_z, over_y)]
    key_grad, value_grad, both = pl.pallas_call(
        finish_kernel,
        out_shape=(jax.ShapeDtypeStruct((tok, hd), BF16),) * 2
        + (jax.ShapeDtypeStruct((tok, 2 * hd), BF16),),
        grid=(1,),
        in_specs=[whole(tables.shape), whole(kv0.shape), hbm]
        + [whole(x.shape) for x in homes],
        out_specs=(whole((tok, hd)), whole((tok, hd)), whole((tok, 2 * hd))),
        compiler_params=params(),
        name="finish_keys",
    )(tables, kv0, q_other, *homes)
    kv_other = exchange(both)

    others = head_axis - 1
    slots = 8 if others == 1 else 2
    full = lambda shape: pl.BlockSpec(shape, lambda j, r: (0, 0))
    mine = lambda shape: pl.BlockSpec(shape, lambda j, r: (r[1], 0))
    which = lambda j, r: r[0] ^ (2 * (j % 4) + j // 4)
    wspec = lambda cols: pl.BlockSpec((eighth, cols), lambda j, r: (which(j, r), 0))
    d_input = pl.pallas_call(
        functools.partial(project_kernel, others, slots),
        out_shape=jax.ShapeDtypeStruct((out_rows, d_model), BF16),
        grid_spec=pltpu.PrefetchScalarGridSpec(
            num_scalar_prefetch=1,
            grid=(8,),
            in_specs=[
                mine((out_rows, col_width)),
                mine((out_rows, hd)),
                mine((out_rows, hd)),
                full((out_rows, col_width * others)),
                full((out_rows, 2 * hd * others)),
                wspec(col_width),
                wspec(hd),
                wspec(hd),
            ]
            + [hbm] * 8,
            out_specs=pl.BlockSpec((out_rows, eighth), lambda j, r: (0, which(j, r))),
            scratch_shapes=[
                pltpu.VMEM((slots, eighth, (col_width + 2 * hd) * others), BF16),
                pltpu.SemaphoreType.DMA((8,)),
            ],
        ),
        compiler_params=params(),
        name="project",
    )(
        spot,
        query_grad,
        key_grad,
        value_grad,
        q_other,
        kv_other,
        q_weight,
        k_weight,
        v_weight,
        *pieces,
    )
    return (d_input, key_grad, value_grad)


def solution(mesh):
    in_specs = (
        P("seq", "head"),
        P("seq", "head"),
        P("seq", "head"),
        P("seq", "head"),
        P("seq", "head"),
        P("head", "seq"),
        P(),
        P(None, "head"),
        P(None, "head"),
        P(None, "head"),
    )
    out_specs = (P(("seq", "head"), None), P("seq", "head"), P("seq", "head"))
    return jax.shard_map(local, mesh=mesh, in_specs=in_specs, out_specs=out_specs, check_vma=False)
```
